128 devices in a mesh: seq: 32 (over y, x, z_hi), grp: 4 (over z_lo, core).
Axes of the slice: x: 4, y: 4, z: 4 (z_hi: 2, z_lo: 2; z = z_hi * 2 + z_lo), core: 2. Of those that a mesh axis runs over, the one named last changes fastest.
Arguments:
- inputs: bfloat16 [4, 8192, 1536], P('grp', 'seq'), may hold values from -6 to 6
- cotangent: bfloat16 [4, 8192, 1536], P('grp', 'seq'), may hold values from -6 to 6
- filter_weight: bfloat16 [4608, 640], replicated, may hold values from -0.09375 to 0.09375
- projection_weight: bfloat16 [640, 1536], replicated, may hold values from -0.25 to 0.25
Outputs:
- input_gradient: bfloat16 [4, 8192, 1536], P('grp', 'seq')
- filter_gradient: float32 [4608, 640], P(('seq', 'grp'))
- projection_gradient: float32 [640, 1536], P(('seq', 'grp'))
The draws below stay inside these ranges and needn't reach their ends.
All inputs are finite; a program needn't handle non-finite values.
Results may differ from the reference program's by a relative error of at most 0.0054.
Values may be sent and summed in bfloat16 or wider, within the bound.
A program may use at most 128 MiB of HBM per device.

```python
import jax
import jax.numpy as jnp
from jax import lax

C = 1536
H = 640
DILATION = 64
LENGTH = 8192
SEQS = 4


def block_levels(key, extent, shards, low, high):
    gain = 1.0
    for position, parts in shards:
        heights = jax.random.uniform(jax.random.fold_in(jax.random.fold_in(key, 6), position), (parts,), jnp.float32, low / len(shards), high / len(shards))
        gain = gain * jnp.repeat(jnp.exp(heights), extent[position] // parts).reshape((-1,) + (1,) * (len(extent) - 1 - position))
    return gain


def centred(rng, dims, deviation, most, shards=(), kind=jnp.bfloat16):
    drawn = jax.random.normal(rng, dims, jnp.float32) * deviation
    if len(shards) > 0:
        drawn = block_levels(rng, dims, shards, -0.22, 0.18) * drawn
    return jnp.clip(drawn, min=-most, max=most).astype(kind)


def setup_inputs(seed: int = 0) -> dict:
    seeds = jax.random.split(jax.random.key(seed), 5)
    return {
        "inputs": centred(seeds[0], (SEQS, LENGTH, C), 1.0, 6.0, ((0, 4), (1, 32))),
        "cotangent": centred(seeds[1], (SEQS, LENGTH, C), 1.0, 6.0, ((0, 4), (1, 32))),
        "filter_weight": centred(seeds[2], (3 * C, H), (3 * C) ** -0.5, 0.09375),
        "projection_weight": centred(seeds[3], (H, C), H ** -0.5, 0.25),
    }


def gelu_fwd(v):
    return jax.nn.gelu(v, approximate=True)


def gelu_slope(v):
    coeff = 0.7978845608028654
    inner = coeff * (v + 0.044715 * v * v * v)
    tanh_val = jnp.tanh(inner)
    return 0.5 * (1.0 + tanh_val) + 0.5 * v * (1.0 - tanh_val * tanh_val) * coeff * (1.0 + 3.0 * 0.044715 * v * v)


def shifted(array, dist):
    length = array.shape[1]
    padded = jnp.pad(array, ((0, 0), (dist, dist), (0, 0)))
    return padded[:, :length], padded[:, 2 * dist:2 * dist + length]


def reference(inputs, cotangent, filter_weight, projection_weight):
    seqs, length, chans = inputs.shape
    hidden = projection_weight.shape[0]
    gradient_scale = 1.0 / (seqs * length) ** 0.5
    act = gelu_fwd(inputs.astype(jnp.float32)).astype(jnp.bfloat16)
    earlier, later = shifted(act, DILATION)
    taps = jnp.concatenate([earlier, act, later], axis=-1).reshape(seqs * length, 3 * chans)
    pre = jnp.dot(taps, filter_weight, preferred_element_type=jnp.float32)
    post = gelu_fwd(pre).astype(jnp.bfloat16)
    flat_up = cotangent.reshape(seqs * length, chans)
    d_post = lax.dot_general(flat_up, projection_weight, (((1,), (1,)), ((), ())), preferred_element_type=jnp.float32)
    d_pre = (d_post * gelu_slope(pre)).astype(jnp.bfloat16)
    projection_gradient = lax.dot_general(post, flat_up, (((0,), (0,)), ((), ())), preferred_element_type=jnp.float32) * gradient_scale
    filter_gradient = lax.dot_general(taps, d_pre, (((0,), (0,)), ((), ())), preferred_element_type=jnp.float32) * gradient_scale
    d_pre3 = d_pre.reshape(seqs, length, hidden)
    before, after = shifted(d_pre3, DILATION)
    pieces = [after, d_pre3, before]
    d_act = jnp.zeros((seqs * length, chans), jnp.float32)
    for k in range(3):
        d_act = d_act + lax.dot_general(pieces[k].reshape(seqs * length, hidden), filter_weight[k * chans:(k + 1) * chans],
                                        (((1,), (1,)), ((), ())), preferred_element_type=jnp.float32)
    input_gradient = (cotangent.astype(jnp.float32) + d_act.reshape(seqs, length, chans) * gelu_slope(inputs.astype(jnp.float32))).astype(jnp.bfloat16)
    return input_gradient, filter_gradient, projection_gradient
```

```python
import jax
import jax.numpy as jnp
from jax import lax
from jax.experimental import pallas as pl
from jax.experimental.pallas import tpu as pltpu
from jax.sharding import PartitionSpec as P

MESH = pl.DeviceIdType.MESH
BF, F32 = jnp.bfloat16, jnp.float32
D = 64
T = 256
C = 1536
H = 640
RA, RB = 1600, 1152
COEFF = 0.7978845608028654
NT = (((1,), (1,)), ((), ()))

S_HALO = 0
S_DZ = 2
S_SIB = 4
S_P1 = 12
S_P2 = 30
S_P3 = 39
N_SEM = 63


def tanh_of(v):
    return jnp.tanh(COEFF * (v + 0.044715 * (v * v * v)))


def slope(v, t):
    return 0.5 * (1.0 + t) + 0.5 * v * (1.0 - t * t) * COEFF * (1.0 + 3.0 * 0.044715 * v * v)


def dot(a, b):
    return jnp.dot(a, b, preferred_element_type=F32)


def dot_nt(a, b):
    return lax.dot_general(a, b, NT, preferred_element_type=F32)


def kernel(x_hbm, cot_hbm, fw_hbm, pw_hbm, ig_hbm, fo_ref, po_ref,
           xe, ue, ut, cot, fw, pw, z_ref, dg_ref, g_ref, gt, dz, dzx, dw,
           pa, pb, pc, rla, rlb, rlc, rfa, rfb, rfc,
           sa, qa, qb, qc, rqa, rqb, rqc, s2a, s2b, s2c, ta, tb, tc, rta, rtb, rtc,
           ig, lsem, ssem, rsem):
    seq, grp = lax.axis_index("seq"), lax.axis_index("grp")
    y, x, z, c = seq // 8, (seq // 2) % 4, (seq % 2) * 2 + grp // 2, grp % 2
    o = 1 - c

    def dev(xx, yy, zz, cc):
        return (yy * 8 + xx * 2 + zz // 2, (zz % 2) * 2 + cc)

    def at(axis, d, cc):
        xx = (x + d) % 4 if axis == "x" else x
        yy = (y + d) % 4 if axis == "y" else y
        zz = (z + d) % 4 if axis == "z" else z
        return dev(xx, yy, zz, cc)

    sibling = (seq, lax.rem(grp, 2) * (-2) + 1 + grp)
    pos = {"x": x, "y": y, "z": z}
    has_prev, has_next = seq > 0, seq < 31

    def remote(src, dst, sem, device):
        return pltpu.make_async_remote_copy(
            src_ref=src, dst_ref=dst, send_sem=ssem.at[sem[0]], recv_sem=rsem.at[sem[1]],
            device_id=device, device_id_type=MESH)

    def local(src, dst, i):
        return pltpu.make_async_copy(src, dst, lsem.at[i])

    load_x = local(x_hbm.at[0], xe.at[pl.ds(D, T)], 0)
    load_f = [local(fw_hbm.at[pl.ds(C * k, C)], fw.at[pl.ds(C * k, C)], 1 + k) for k in range(3)]
    load_c = local(cot_hbm.at[0], cot.at[pl.ds(0, T)], 4)
    load_p = local(pw_hbm, pw, 5)
    load_x.start()
    load_f[1].start()
    load_f[0].start()
    load_f[2].start()
    load_c.start()
    load_p.start()

    barrier = pltpu.get_barrier_semaphore()

    def greet(device):
        pl.semaphore_signal(barrier, inc=1, device_id=device, device_id_type=MESH)

    greet(sibling)
    for axis in ("x", "y", "z"):
        for d in (1, 2, 3):
            for cc in (0, 1):
                greet(at(axis, d, cc))
    nxt, prv = (seq + 1, grp), (seq - 1, grp)

    @pl.when(has_next)
    def _():
        greet(nxt)

    @pl.when(has_prev)
    def _():
        greet(prv)

    pl.semaphore_wait(barrier, 19 + has_prev.astype(jnp.int32) + has_next.astype(jnp.int32))

    halo_up = remote(x_hbm.at[0, pl.ds(T - D, D)], xe.at[pl.ds(0, D)], (S_HALO, S_HALO), nxt)
    halo_dn = remote(x_hbm.at[0, pl.ds(0, D)], xe.at[pl.ds(D + T, D)], (S_HALO + 1, S_HALO + 1), prv)
    dz_up = remote(dzx.at[pl.ds(T, D)], dzx.at[pl.ds(0, D)], (S_DZ, S_DZ), nxt)
    dz_dn = remote(dzx.at[pl.ds(D, D)], dzx.at[pl.ds(D + T, D)], (S_DZ + 1, S_DZ + 1), prv)

    @pl.when(has_next)
    def _():
        halo_up.start()

    @pl.when(has_prev)
    def _():
        halo_dn.start()

    sib_c = remote(cot_hbm.at[0], cot.at[pl.ds(T, T)], (S_SIB, S_SIB), sibling)
    sib_u = [remote(ut.at[0, i], ut.at[1, i], (S_SIB + 1 + i, S_SIB + 1 + i), sibling) for i in range(4)]
    sib_g = remote(gt.at[0], gt.at[1], (S_SIB + 5, S_SIB + 5), sibling)
    sib_d = remote(dz.at[0], dz.at[1], (S_SIB + 6, S_SIB + 6), sibling)
    sib_c.start()

    def act(start, rows):
        v = xe[pl.ds(start, rows)].astype(F32)
        ue[pl.ds(start, rows)] = (0.5 * v * (1.0 + tanh_of(v))).astype(BF)

    load_x.wait()

    @pl.loop(0, T // 32)
    def _(i):
        act(pl.multiple_of(D + i * 32, 32), 32)

    ut[0, 0] = ue[128:256].T
    ut[0, 2] = jnp.concatenate([ue[64:128], ue[256:320]], axis=0).T
    sib_u[0].start()
    sib_u[2].start()

    load_f[1].wait()
    z_ref[...] = dot(ue[64:320], fw[C:2 * C])
    load_f[0].wait()
    z_ref[64:256] += dot(ue[64:256], fw[0:C])
    load_f[2].wait()
    z_ref[0:192] += dot(ue[128:320], fw[2 * C:3 * C])
    load_c.wait()
    load_p.wait()
    dg_ref[...] = dot_nt(cot[0:T], pw[...])

    @pl.when(has_prev)
    def _():
        halo_up.wait_recv()
        act(0, 32)
        act(32, 32)

    @pl.when(jnp.logical_not(has_prev))
    def _():
        ue[0:D] = jnp.zeros((D, C), BF)

    @pl.when(has_next)
    def _():
        halo_dn.wait_recv()
        act(D + T, 32)
        act(D + T + 32, 32)

    @pl.when(jnp.logical_not(has_next))
    def _():
        ue[D + T:D + T + D] = jnp.zeros((D, C), BF)

    z_ref[0:64] += dot(ue[0:64], fw[0:C])
    z_ref[192:256] += dot(ue[320:384], fw[2 * C:3 * C])
    ut[0, 1] = ue[0:128].T
    ut[0, 3] = ue[256:384].T
    sib_u[1].start()
    sib_u[3].start()

    @pl.loop(0, T // 32)
    def _(i):
        rows = pl.ds(pl.multiple_of(i * 32, 32), 32)
        v = z_ref[rows]
        t = tanh_of(v)
        g_ref[rows] = (0.5 * v * (1.0 + t)).astype(BF)
        d = (dg_ref[rows] * slope(v, t)).astype(BF)
        dz[0, rows] = d
        dzx[pl.ds(pl.multiple_of(D + i * 32, 32), 32)] = d

    gt[0] = g_ref[...].T
    sib_g.start()
    sib_d.start()

    @pl.when(has_next)
    def _():
        dz_up.start()

    @pl.when(has_prev)
    def _():
        dz_dn.start()

    rings = {
        "A": ("y", lambda j, h: pa.at[j, pl.ds(RA // 2 * h, RA // 2)], rla, rfa, S_P1),
        "B": ("x", lambda j, h: pb.at[j, pl.ds(2 * h, 2)], rlb, rfb, S_P1 + 6),
        "C": ("z", lambda j, h: pc.at[j, pl.ds(2 * h, 2)], rlc, rfc, S_P1 + 12),
    }

    def ring(part):
        axis, chunk, rl, rf, sem = rings[part]
        i = pos[axis]
        up, far, dn = (i + 1) % 4, (i + 2) % 4, (i + 3) % 4
        out = []
        for k, (near, h, to) in enumerate(((up, 0, 1), (dn, 1, 3))):
            who = at(axis, to, c)
            s = sem + 3 * k
            out.append((
                remote(chunk(far, h), rl.at[k], (s, s), who),
                remote(chunk(near, 1 - h), rf.at[k, 0], (s + 1, s + 1), who),
                remote(chunk(near, h), rf.at[k, 1], (s + 2, s + 2), who),
                chunk(near, h), rl.at[k]))
        return out

    steps = {part: ring(part) for part in rings}

    def ring_start(part):
        for which in (0, 1):
            for k in (0, 1):
                steps[part][k][which].start()

    def ring_relay(part):
        for k in (0, 1):
            first, _, second, mine, came = steps[part][k]
            first.wait_recv()
            mine[...] = (mine[...].astype(F32) + came[...].astype(F32)).astype(BF)
            second.start()

    def ring_end(part):
        for k in (0, 1):
            steps[part][k][1].wait_recv()
            steps[part][k][2].wait_recv()

    sib_g.wait_recv()
    sib_c.wait_recv()

    @pl.loop(0, jnp.where(c == 0, 1, 5))
    def _(i):
        col = pl.multiple_of(256 * (i + c), 256)
        acc = dot(gt[0], cot[0:T, pl.ds(col, 256)]) + dot(gt[1], cot[T:2 * T, pl.ds(col, 256)])
        for j in range(4):
            for b in range(2):
                pa[j, pl.ds(pl.multiple_of(320 * i + 160 * b, 160), 160)] = (
                    acc[160 * j:160 * (j + 1), 128 * b:128 * (b + 1)].astype(BF))

    @pl.when(c == 1)
    def _():
        ring_start("A")

    sib_d.wait_recv()
    order = ((2, 3, 0, 1), (1, 2, 0, 3), (0, 1, 2, 3))
    col = pl.multiple_of(256 * c, 256)
    for k in range(3):
        for s in range(2):
            for b in range(4):
                src = pl.ds(64 * order[k][b], 64)
                dst = pl.ds(256 * s + 64 * b, 64)
                dw[k, dst, 0:256] = dz[s, src, pl.ds(col, 256)]
                dw[k, dst, 256:384] = dz[s, src, 512:640]
    for i in range(4):
        sib_u[i].wait_recv()

    def lhs(unit):
        tap, first = unit // 8, pl.ds(pl.multiple_of((unit % 8) * 192, 192), 192)
        return tap, jnp.concatenate(
            [ut[0, 0, first], ut[0, 1 + tap_tile(tap), first],
             ut[1, 0, first], ut[1, 1 + tap_tile(tap), first]], axis=1)

    def tap_tile(tap):
        return tap

    @pl.loop(0, 8)
    def _(g):
        yy, xp = g // 2, g % 2
        parts = []
        for q in range(3):
            tap, left = lhs(3 * g + q)
            parts.append(dot(left, dw[tap, :, 0:256]))
        acc = jnp.concatenate(parts, axis=0)
        pb[2 * xp, yy] = acc[0:288, 0:128].astype(BF)
        pb[2 * xp + 1, yy] = acc[288:576, 0:128].astype(BF)
        for zz in range(4):
            pc[zz, yy, xp] = jnp.concatenate(
                [acc[72 * zz:72 * zz + 72, 128:256], acc[288 + 72 * zz:360 + 72 * zz, 128:256]],
                axis=0).astype(BF)

    ring_start("B")
    ring_start("C")

    @pl.when(c == 0)
    def _():
        @pl.loop(0, 8)
        def _(g):
            yy, xp = g // 2, g % 2
            for q in range(3):
                tap, left = lhs(3 * g + q)
                row = pl.multiple_of(320 + 576 * xp + 192 * q, 64)
                pa[yy, pl.ds(row, 192)] = dot(left, dw[tap, :, 256:384]).astype(BF)

        ring_start("A")

    @pl.when(has_prev)
    def _():
        dz_up.wait_recv()

    @pl.when(jnp.logical_not(has_prev))
    def _():
        dzx[0:D] = jnp.zeros((D, H), BF)

    @pl.when(has_next)
    def _():
        dz_dn.wait_recv()

    @pl.when(jnp.logical_not(has_next))
    def _():
        dzx[D + T:D + T + D] = jnp.zeros((D, H), BF)

    def du(lo, hi):
        @pl.loop(lo, hi)
        def _(n):
            cols = pl.ds(pl.multiple_of(256 * n, 256), 256)
            acc = jnp.zeros((T, 256), F32)
            for k in range(3):
                rows = pl.ds(pl.multiple_of(C * k + 256 * n, 256), 256)
                acc += dot_nt(dzx[D * (2 - k):D * (2 - k) + T], fw[rows])
            v = xe[D:D + T, cols].astype(F32)
            ig[:, cols] = (cot[0:T, cols].astype(F32) + acc * slope(v, tanh_of(v))).astype(BF)

    ring_relay("B")
    ring_relay("C")
    ring_relay("A")
    du(0, 3)

    def second(part, axis, q, rq, sem):
        return [remote(q.at[(pos[axis] + d) % 4], rq.at[d - 1], (sem + d - 1, sem + d - 1), at(axis, d, c))
                for d in (1, 2, 3)]

    sec_a = second("A", "x", qa, rqa, S_P2)
    sec_b = second("B", "z", qb, rqb, S_P2 + 3)
    sec_c = second("C", "y", qc, rqc, S_P2 + 6)

    def up32(v):
        return v.astype(F32)

    ring_end("B")
    for h in range(2):
        s = up32(pb[x, pl.ds(2 * h, 2)]) + up32(rfb[0, 1 - h]) + up32(rfb[1, h])
        for zz in range(4):
            qb[zz, pl.ds(144 * h, 144)] = jnp.concatenate(
                [s[0, 72 * zz:72 * zz + 72], s[1, 72 * zz:72 * zz + 72]], axis=0).astype(BF)
    for cp in sec_b:
        cp.start()

    ring_end("C")
    for h in range(2):
        s = up32(pc[z, pl.ds(2 * h, 2)]) + up32(rfc[0, 1 - h]) + up32(rfc[1, h])
        for yy in range(2):
            for xp in range(2):
                qc[2 * h + yy, pl.ds(144 * xp, 144)] = s[yy, xp].astype(BF)
    for cp in sec_c:
        cp.start()

    ring_end("A")
    for h in range(2):
        sa[pl.ds(800 * h, 800)] = (
            up32(pa[y, pl.ds(800 * h, 800)]) + up32(rfa[0, 1 - h]) + up32(rfa[1, h]))

    def pair(p):
        for xx in range(4):
            lo = 320 * p + 40 * xx
            qa[xx, pl.ds(80 * p, 80)] = jnp.concatenate(
                [sa[lo:lo + 40], sa[lo + 160:lo + 200]], axis=0).astype(BF)

    pair(0)

    @pl.when(c == 0)
    def _():
        for xx in range(4):
            qa[xx, 80:368] = sa[320 + 288 * xx:608 + 288 * xx].astype(BF)
            qa[xx, 368:400] = jnp.zeros((32, 128), BF)

    @pl.when(c == 1)
    def _():
        for p in range(1, 5):
            pair(p)

    for cp in sec_a:
        cp.start()

    du(3, 6)
    store_ig = local(ig, ig_hbm.at[0], 6)
    store_ig.start()

    def third(axis, t, rt, sem):
        i = pos[axis]
        out = []
        for d in (1, 2, 3):
            for cc in (0, 1):
                out.append(remote(t.at[(i + d) % 4, cc], rt.at[c, d],
                                  (sem + 4 * cc + d, sem + 4 * c + d), at(axis, d, cc)))
        out.append(remote(t.at[i, o], rt.at[c, 0], (sem + 4 * o, sem + 4 * c), sibling))
        wait = []
        for s in (0, 1):
            for d in (1, 2, 3):
                wait.append(remote(t.at[0, 0], rt.at[s, d], (sem + 4 * s + d, sem + 4 * s + d), sibling))
        wait.append(remote(t.at[0, 0], rt.at[o, 0], (sem + 4 * o, sem + 4 * o), sibling))
        return out, wait

    thr_a = third("z", ta, rta, S_P3)
    thr_b = third("y", tb, rtb, S_P3 + 8)
    thr_c = third("x", tc, rtc, S_P3 + 16)

    def gather(sec, q, rq, mine, s2, rows):
        for cp in sec:
            cp.wait_recv()
        s2[0:rows] = up32(q[mine]) + up32(rq[0]) + up32(rq[1]) + up32(rq[2])

    def rows36(s2, t, i, first, at_row):
        for cc in range(2):
            lo = first + 72 * i + 36 * cc
            t[i, cc, at_row:at_row + 48] = s2[lo:lo + 48].astype(BF)

    s2b[288:304] = jnp.zeros((16, 128), F32)
    s2c[288:304] = jnp.zeros((16, 128), F32)
    s2a[400:408] = jnp.zeros((8, 128), F32)
    for sec, thr, q, rq, mine, s2, t, rt, i in (
            (sec_b, thr_b, qb, rqb, z, s2b, tb, rtb, y), (sec_c, thr_c, qc, rqc, y, s2c, tc, rtc, x)):
        gather(sec, q, rq, mine, s2, 288)
        for n in range(4):
            rows36(s2, t, n, 0, 0)
        for cp in thr[0]:
            cp.start()
        rt[c, 0] = t[i, c]

    gather(sec_a, qa, rqa, x, s2a, 400)

    def fives(p):
        for n in range(4):
            for cc in range(2):
                lo = 80 * p + 10 * n + 5 * cc
                ta[n, cc, pl.ds(16 * p, 16)] = jnp.concatenate(
                    [s2a[lo:lo + 8], s2a[lo + 40:lo + 48]], axis=0).astype(BF)

    fives(0)

    @pl.when(c == 0)
    def _():
        for n in range(4):
            rows36(s2a, ta, n, 80, 16)
            for cc in range(2):
                ta[n, cc, 64:80] = jnp.zeros((16, 128), BF)

    @pl.when(c == 1)
    def _():
        for p in range(1, 5):
            fives(p)

    for cp in thr_a[0]:
        cp.start()
    rta[c, 0] = ta[z, c]

    scale = 1.0 / (4 * 8192) ** 0.5

    def total(rt, s):
        return (up32(rt[s, 0]) + up32(rt[s, 1]) + up32(rt[s, 2]) + up32(rt[s, 3])) * scale

    for cp in thr_b[1]:
        cp.wait_recv()
    for s in range(2):
        fo_ref[:, 256 * s:256 * s + 128] = total(rtb, s)[0:36]
    for cp in thr_c[1]:
        cp.wait_recv()
    for s in range(2):
        fo_ref[:, 256 * s + 128:256 * s + 256] = total(rtc, s)[0:36]
    for cp in thr_a[1]:
        cp.wait_recv()
    low = total(rta, 0)
    fo_ref[:, 512:640] = low[16:52]
    for b in range(2):
        po_ref[:, 128 * b:128 * b + 128] = low[8 * b:8 * b + 5]
    high = total(rta, 1)
    for b in range(10):
        po_ref[:, 128 * (b + 2):128 * (b + 3)] = high[8 * b:8 * b + 5]

    @pl.when(has_next)
    def _():
        halo_up.wait_send()
        dz_up.wait_send()

    @pl.when(has_prev)
    def _():
        halo_dn.wait_send()
        dz_dn.wait_send()

    for cp in [sib_c, sib_g, sib_d] + sib_u:
        cp.wait_send()
    for part in rings:
        for k in (0, 1):
            for w in range(3):
                steps[part][k][w].wait_send()
    for cp in sec_a + sec_b + sec_c + thr_a[0] + thr_b[0] + thr_c[0]:
        cp.wait_send()
    store_ig.wait()


def shards(inputs, cotangent, filter_weight, projection_weight):
    v = pltpu.VMEM
    anywhere = pl.BlockSpec(memory_space=pl.ANY)
    whole = pl.BlockSpec(memory_space=pltpu.VMEM)
    scratch = [
        v((T + 2 * D, C), BF), v((T + 2 * D, C), BF), v((2, 4, C, 128), BF), v((2 * T, C), BF),
        v((3 * C, H), BF), v((H, C), BF), v((T, H), F32), v((T, H), F32), v((T, H), BF),
        v((2, H, T), BF), v((2, T, H), BF), v((T + 2 * D, H), BF), v((3, 2 * T, 384), BF),
        v((4, RA, 128), BF), v((4, 4, 288, 128), BF), v((4, 4, 2, 144, 128), BF),
        v((2, RA // 2, 128), BF), v((2, 2, 288, 128), BF), v((2, 2, 2, 144, 128), BF),
        v((2, 2, RA // 2, 128), BF), v((2, 2, 2, 288, 128), BF), v((2, 2, 2, 2, 144, 128), BF),
        v((RA, 128), F32), v((4, 400, 128), BF), v((4, 288, 128), BF), v((4, 288, 128), BF),
        v((3, 400, 128), BF), v((3, 288, 128), BF), v((3, 288, 128), BF),
        v((408, 128), F32), v((304, 128), F32), v((304, 128), F32),
        v((4, 2, 80, 128), BF), v((4, 2, 48, 128), BF), v((4, 2, 48, 128), BF),
        v((2, 4, 80, 128), BF), v((2, 4, 48, 128), BF), v((2, 4, 48, 128), BF),
        v((T, C), BF),
        pltpu.SemaphoreType.DMA((8,)), pltpu.SemaphoreType.DMA((N_SEM,)), pltpu.SemaphoreType.DMA((N_SEM,)),
    ]
    return pl.pallas_call(
        kernel,
        name="block_backward",
        out_shape=(
            jax.ShapeDtypeStruct((1, T, C), BF),
            jax.ShapeDtypeStruct((36, H), F32),
            jax.ShapeDtypeStruct((5, C), F32),
        ),
        in_specs=[anywhere] * 4,
        out_specs=(anywhere, whole, whole),
        scratch_shapes=scratch,
        compiler_params=pltpu.CompilerParams(
            collective_id=0, has_side_effects=True, vmem_limit_bytes=56 * 2**20),
        cost_estimate=pl.CostEstimate(flops=5_600_000_000, bytes_accessed=12_000_000, transcendentals=1_000_000),
    )(inputs, cotangent, filter_weight, projection_weight)


def solution(mesh):
    in_specs = (P("grp", "seq", None), P("grp", "seq", None), P(), P())
    out_specs = (P("grp", "seq", None), P(("seq", "grp"), None), P(("seq", "grp"), None))
    return jax.shard_map(shards, mesh=mesh, in_specs=in_specs, out_specs=out_specs, check_vma=False)
```

```python
import jax
import jax.numpy as jnp
from jax import lax
from jax.experimental import pallas as pl
from jax.experimental.pallas import tpu as pltpu
from jax.sharding import PartitionSpec as P

MESH = pl.DeviceIdType.MESH
BF, F32 = jnp.bfloat16, jnp.float32
D = 64
T = 256
C = 1536
H = 640
COEFF = 0.7978845608028654
NT = (((1,), (1,)), ((), ()))

S_HALO = 0
S_DZ = 2
S_SIB = 4
S_P1 = 10
S_P2 = 34
S_P3 = 46
N_SEM = 78


def tanh_of(v):
    return jnp.tanh(COEFF * (v + 0.044715 * (v * v * v)))


def slope(v, t):
    return 0.5 * (1.0 + t) + 0.5 * v * (1.0 - t * t) * COEFF * (1.0 + 3.0 * 0.044715 * v * v)


def dot(a, b):
    return jnp.dot(a, b, preferred_element_type=F32)


def dot_nt(a, b):
    return lax.dot_general(a, b, NT, preferred_element_type=F32)


def up32(v):
    return v.astype(F32)


def kernel(x_hbm, cot_hbm, fw_hbm, pw_hbm, ig_hbm, fo_ref, po_ref,
           xv, ue, ut, cot, fw, pw, eo, ei, z_ref, dg_ref, g_ref, gt, dzx, dzc,
           pa, pf, pb, pc, rla, rlf, rlb, rlc, rfa, rff, rfb, rfc,
           sa, sf, qa, qf, qb, qc, rqa, rqf, rqb, rqc, s2a, s2f, s2b, s2c,
           ta, tf, tb, tc, rta, rtf, rtb, rtc, ig, lsem, ssem, rsem):
    seq, grp = lax.axis_index("seq"), lax.axis_index("grp")
    y, x, z, c = seq // 8, (seq // 2) % 4, (seq % 2) * 2 + grp // 2, grp % 2
    o = 1 - c

    def dev(xx, yy, zz, cc):
        return (yy * 8 + xx * 2 + zz // 2, (zz % 2) * 2 + cc)

    def at(axis, d, cc):
        xx = (x + d) % 4 if axis == "x" else x
        yy = (y + d) % 4 if axis == "y" else y
        zz = (z + d) % 4 if axis == "z" else z
        return dev(xx, yy, zz, cc)

    sibling = (seq, grp + 1 - 2 * c)
    pos = {"x": x, "y": y, "z": z}
    has_prev, has_next = seq > 0, seq < 31
    nxt, prv = (seq + 1, grp), (seq - 1, grp)

    def remote(src, dst, sem, device):
        return pltpu.make_async_remote_copy(
            src_ref=src, dst_ref=dst, send_sem=ssem.at[sem[0]], recv_sem=rsem.at[sem[1]],
            device_id=device, device_id_type=MESH)

    def local(src, dst, i):
        return pltpu.make_async_copy(src, dst, lsem.at[i])

    load_x = local(x_hbm.at[0], xv, 0)
    load_f = [local(fw_hbm.at[pl.ds(C * k, C)], fw.at[pl.ds(C * k, C)], 1 + k) for k in range(3)]
    load_c = local(cot_hbm.at[0], cot.at[pl.ds(0, T)], 4)
    load_p = local(pw_hbm, pw, 5)
    load_x.start()
    load_f[0].start()
    load_f[2].start()

    barrier = pltpu.get_barrier_semaphore()

    def greet(device):
        pl.semaphore_signal(barrier, inc=1, device_id=device, device_id_type=MESH)

    @pl.when(has_next)
    def _():
        greet(nxt)

    @pl.when(has_prev)
    def _():
        greet(prv)

    greet(sibling)
    for axis in ("x", "y", "z"):
        for d in (1, 2, 3):
            for cc in (0, 1):
                greet(at(axis, d, cc))

    def act(first, rows):
        v = up32(xv[pl.ds(first, rows)])
        ue[pl.ds(first, rows)] = (0.5 * v * (1.0 + tanh_of(v))).astype(BF)

    load_x.wait()
    for first in (192, 224, 0, 32):
        act(first, 32)
    load_f[0].wait()
    eo[0] = dot(ue[T - D:T], fw[0:C]).astype(BF)
    load_f[2].wait()
    load_f[1].start()
    load_c.start()
    load_p.start()
    eo[1] = dot(ue[0:D], fw[2 * C:3 * C]).astype(BF)

    pl.semaphore_wait(barrier, 19 + has_prev.astype(jnp.int32) + has_next.astype(jnp.int32))

    halo_up = remote(eo.at[0], ei.at[0], (S_HALO, S_HALO), nxt)
    halo_dn = remote(eo.at[1], ei.at[1], (S_HALO + 1, S_HALO + 1), prv)
    dz_up = remote(dzx.at[0, pl.ds(T, D)], dzx.at[0, pl.ds(0, D)], (S_DZ, S_DZ), nxt)
    dz_dn = remote(dzx.at[0, pl.ds(D, D)], dzx.at[0, pl.ds(D + T, D)], (S_DZ + 1, S_DZ + 1), prv)

    @pl.when(has_next)
    def _():
        halo_up.start()

    @pl.when(has_prev)
    def _():
        halo_dn.start()

    sib_c = remote(cot_hbm.at[0], cot.at[pl.ds(T, T)], (S_SIB, S_SIB), sibling)
    sib_u = remote(ut.at[0], ut.at[1], (S_SIB + 1, S_SIB + 1), sibling)
    sib_g = remote(gt.at[0], gt.at[1], (S_SIB + 2, S_SIB + 2), sibling)

    def sib_dz(first, rows, sem):
        return remote(dzx.at[0, pl.ds(first, rows)], dzx.at[1, pl.ds(first, rows)], (sem, sem), sibling)

    sib_d = sib_dz(D, T, S_SIB + 3)
    sib_lo = sib_dz(0, D, S_SIB + 4)
    sib_hi = sib_dz(D + T, D, S_SIB + 5)
    sib_c.start()

    @pl.loop(0, 4)
    def _(i):
        act(pl.multiple_of(D + i * 32, 32), 32)

    ut[0, :, 0:128] = ue[0:128].T
    ut[0, :, 128:256] = ue[128:256].T
    sib_u.start()

    load_f[1].wait()
    z_ref[...] = dot(ue[...], fw[C:2 * C])
    z_ref[64:256] += dot(ue[0:192], fw[0:C])
    z_ref[0:192] += dot(ue[64:256], fw[2 * C:3 * C])
    load_c.wait()
    load_p.wait()
    dg_ref[...] = dot_nt(cot[0:T], pw[...])

    def inner(first):
        rows = pl.ds(first, 32)
        v = z_ref[rows]
        t = tanh_of(v)
        g_ref[rows] = (0.5 * v * (1.0 + t)).astype(BF)
        dzx[0, pl.ds(D + first, 32)] = (dg_ref[rows] * slope(v, t)).astype(BF)

    for first in (64, 96, 128, 160):
        inner(first)

    @pl.when(has_prev)
    def _():
        halo_up.wait_recv()
        z_ref[0:64] += up32(ei[0])

    @pl.when(has_next)
    def _():
        halo_dn.wait_recv()
        z_ref[192:256] += up32(ei[1])

    for first in (0, 32, 192, 224):
        inner(first)

    @pl.when(has_next)
    def _():
        dz_up.start()

    @pl.when(has_prev)
    def _():
        dz_dn.start()

    gt[0] = g_ref[...].T
    sib_g.start()
    sib_d.start()

    rings = {
        "A": ("y", lambda j, h: pa.at[j, pl.ds(320 * h, 320)], rla, rfa, S_P1),
        "F": ("y", lambda j, h: pf.at[j, pl.ds(576 * h, 576)], rlf, rff, S_P1 + 6),
        "G": ("y", lambda j, h: pf.at[j, pl.ds(320 * h, 320)], rlf.at[:, 0:320], rff.at[:, :, 0:320], S_P1 + 6),
        "B": ("x", lambda j, h: pb.at[j, pl.ds(2 * h, 2)], rlb, rfb, S_P1 + 12),
        "C": ("z", lambda j, h: pc.at[j, pl.ds(2 * h, 2)], rlc, rfc, S_P1 + 18),
    }

    def ring(part):
        axis, chunk, rl, rf, sem = rings[part]
        i = pos[axis]
        up, far, dn = (i + 1) % 4, (i + 2) % 4, (i + 3) % 4
        out = []
        for k, (near, h, to) in enumerate(((up, 0, 1), (dn, 1, 3))):
            who = at(axis, to, c)
            s = sem + 3 * k
            out.append((
                remote(chunk(far, h), rl.at[k], (s, s), who),
                remote(chunk(near, 1 - h), rf.at[k, 0], (s + 1, s + 1), who),
                remote(chunk(near, h), rf.at[k, 1], (s + 2, s + 2), who),
                chunk(near, h), rl.at[k]))
        return out

    steps = {part: ring(part) for part in rings}

    def ring_start(part):
        for which in (0, 1):
            for k in (0, 1):
                steps[part][k][which].start()

    def ring_relay(part):
        for k in (0, 1):
            first, _, second, mine, came = steps[part][k]
            first.wait_recv()
            mine[...] = (up32(mine[...]) + up32(came[...])).astype(BF)
            second.start()

    def ring_end(part):
        for k in (0, 1):
            steps[part][k][1].wait_recv()
            steps[part][k][2].wait_recv()

    def proj(to, first, n):
        cols = pl.ds(pl.multiple_of(first, 256), 256)
        acc = dot(gt[0], cot[0:T, cols]) + dot(gt[1], cot[T:2 * T, cols])
        for j in range(4):
            for b in range(2):
                to[j, 320 * n + 160 * b:320 * n + 160 * (b + 1)] = (
                    acc[160 * j:160 * (j + 1), 128 * b:128 * (b + 1)].astype(BF))

    sib_c.wait_recv()
    sib_g.wait_recv()
    for n in range(2):
        proj(pa, 512 * c + 256 * n, n)
    ring_start("A")

    @pl.when(c == 1)
    def _():
        for n in range(2):
            proj(pf, 1024 + 256 * n, n)
        ring_start("G")

    def columns(s, first, rows):
        r = pl.ds(first, rows)
        dzc[s, r, 0:256] = dzx[s, r, pl.ds(pl.multiple_of(256 * c, 256), 256)]
        dzc[s, r, 256:384] = dzx[s, r, 512:640]

    def rhs(tap, lo, hi):
        r = pl.ds(D * (2 - tap), T)
        return jnp.concatenate([dzc[0, r, lo:hi], dzc[1, r, lo:hi]], axis=0)

    def rows_of(first, rows, lo, hi):
        out = []
        last = first + rows
        while first < last:
            tap = first // C
            stop = min(last, C * (tap + 1))
            r = slice(first - C * tap, stop - C * tap)
            left = jnp.concatenate([ut[0, r], ut[1, r]], axis=1)
            out.append(dot(left, rhs(tap, lo, hi)))
            first = stop
        return out[0] if len(out) == 1 else jnp.concatenate(out, axis=0)

    def filt(n):
        yy, xp = n // 2, n % 2
        acc = rows_of(576 * n, 576, 0, 256)
        pb[2 * xp, yy] = acc[0:288, 0:128].astype(BF)
        pb[2 * xp + 1, yy] = acc[288:576, 0:128].astype(BF)
        for zz in range(4):
            pc[zz, yy, xp] = jnp.concatenate(
                [acc[72 * zz:72 * zz + 72, 128:256], acc[288 + 72 * zz:360 + 72 * zz, 128:256]],
                axis=0).astype(BF)

    columns(0, D, T)
    sib_u.wait_recv()
    sib_d.wait_recv()
    columns(1, D, T)
    filt(3)
    filt(4)
    @pl.when(has_prev)
    def _():
        dz_up.wait_recv()

    @pl.when(jnp.logical_not(has_prev))
    def _():
        dzx[0, 0:D] = jnp.zeros((D, H), BF)

    sib_lo.start()

    @pl.when(has_next)
    def _():
        dz_dn.wait_recv()

    @pl.when(jnp.logical_not(has_next))
    def _():
        dzx[0, D + T:D + T + D] = jnp.zeros((D, H), BF)

    sib_hi.start()
    columns(0, 0, D)
    columns(0, D + T, D)
    ring_relay("A")
    sib_lo.wait_recv()
    sib_hi.wait_recv()
    columns(1, 0, D)
    columns(1, D + T, D)
    for n in (0, 1, 2, 5, 6, 7):
        filt(n)
    ring_start("B")
    ring_start("C")

    @pl.when(c == 0)
    def _():
        for n in range(8):
            pf[n // 2, 576 * (n % 2):576 * (n % 2 + 1)] = rows_of(576 * n, 576, 256, 384).astype(BF)
        ring_start("F")

    def du(lo, hi):
        @pl.loop(lo, hi)
        def _(n):
            cols = pl.ds(pl.multiple_of(256 * n, 256), 256)
            acc = jnp.zeros((T, 256), F32)
            for k in range(3):
                rows = pl.ds(pl.multiple_of(C * k + 256 * n, 256), 256)
                acc += dot_nt(dzx[0, D * (2 - k):D * (2 - k) + T], fw[rows])
            v = up32(xv[:, cols])
            ig[:, cols] = (up32(cot[0:T, cols]) + acc * slope(v, tanh_of(v))).astype(BF)

    def second(axis, q, rq, sem):
        return [remote(q.at[(pos[axis] + d) % 4], rq.at[d - 1], (sem + d - 1, sem + d - 1), at(axis, d, c))
                for d in (1, 2, 3)]

    sec_a = second("x", qa, rqa, S_P2)
    sec_f = second("x", qf, rqf, S_P2 + 3)
    sec_b = second("z", qb, rqb, S_P2 + 6)
    sec_c = second("y", qc, rqc, S_P2 + 9)

    def third(axis, t, rt, sem):
        i = pos[axis]
        out = []
        for d in (2, 1, 3):
            for cc in (0, 1):
                out.append(remote(t.at[(i + d) % 4, cc], rt.at[c, d],
                                  (sem + 4 * cc + d, sem + 4 * c + d), at(axis, d, cc)))
        out.append(remote(t.at[i, o], rt.at[c, 0], (sem + 4 * o, sem + 4 * c), sibling))
        wait = []
        for s in (0, 1):
            for d in (1, 2, 3):
                wait.append(remote(t.at[0, 0], rt.at[s, d], (sem + 4 * s + d, sem + 4 * s + d), sibling))
        wait.append(remote(t.at[0, 0], rt.at[o, 0], (sem + 4 * o, sem + 4 * o), sibling))
        return out, wait

    thr_a = third("z", ta, rta, S_P3)
    thr_f = third("z", tf, rtf, S_P3 + 8)
    thr_b = third("y", tb, rtb, S_P3 + 16)
    thr_c = third("x", tc, rtc, S_P3 + 24)

    def begin(copies):
        for cp in copies:
            cp.start()

    def pairs(q, s):
        for p in range(2):
            for xx in range(4):
                lo = 320 * p + 40 * xx
                q[xx, 80 * p:80 * (p + 1)] = jnp.concatenate(
                    [s[lo:lo + 40], s[lo + 160:lo + 200]], axis=0).astype(BF)

    def gather(sec, q, rq, mine, s2, rows):
        for cp in sec:
            cp.wait_recv()
        s2[0:rows] = up32(q[mine]) + up32(rq[0]) + up32(rq[1]) + up32(rq[2])

    def rows36(s2, t):
        for n in range(4):
            for cc in range(2):
                lo = 72 * n + 36 * cc
                t[n, cc] = s2[lo:lo + 48].astype(BF)

    def fives(s2, t):
        for p in range(2):
            for n in range(4):
                for cc in range(2):
                    lo = 80 * p + 10 * n + 5 * cc
                    t[n, cc, 16 * p:16 * (p + 1)] = jnp.concatenate(
                        [s2[lo:lo + 8], s2[lo + 40:lo + 48]], axis=0).astype(BF)

    @pl.when(c == 1)
    def _():
        ring_relay("G")

    du(0, 3)
    ring_relay("B")
    ring_relay("C")

    @pl.when(c == 0)
    def _():
        ring_relay("F")
    ring_end("A")
    for h in range(2):
        sa[320 * h:320 * (h + 1)] = up32(pa[y, 320 * h:320 * (h + 1)]) + up32(rfa[0, 1 - h]) + up32(rfa[1, h])
    pairs(qa, sa)
    begin(sec_a)


    s2a[160:168] = jnp.zeros((8, 128), F32)
    s2f[288:304] = jnp.zeros((16, 128), F32)
    s2b[288:304] = jnp.zeros((16, 128), F32)
    s2c[288:304] = jnp.zeros((16, 128), F32)
    ring_end("B")
    for h in range(2):
        s = up32(pb[x, pl.ds(2 * h, 2)]) + up32(rfb[0, 1 - h]) + up32(rfb[1, h])
        for zz in range(4):
            qb[zz, pl.ds(144 * h, 144)] = jnp.concatenate(
                [s[0, 72 * zz:72 * zz + 72], s[1, 72 * zz:72 * zz + 72]], axis=0).astype(BF)
    begin(sec_b)

    ring_end("C")
    for h in range(2):
        s = up32(pc[z, pl.ds(2 * h, 2)]) + up32(rfc[0, 1 - h]) + up32(rfc[1, h])
        for yy in range(2):
            for xp in range(2):
                qc[2 * h + yy, pl.ds(144 * xp, 144)] = s[yy, xp].astype(BF)
    begin(sec_c)

    def sum_f(rows):
        for h in range(2):
            r = pl.ds(rows * h, rows)
            sf[r] = up32(pf[y, r]) + up32(rff[0, 1 - h, 0:rows]) + up32(rff[1, h, 0:rows])

    @pl.when(c == 0)
    def _():
        ring_end("F")
        sum_f(576)
        for xx in range(4):
            qf[xx] = sf[288 * xx:288 * (xx + 1)].astype(BF)

    @pl.when(c == 1)
    def _():
        ring_end("G")
        sum_f(320)
        pairs(qf, sf)
        for xx in range(4):
            qf[xx, 160:288] = jnp.zeros((128, 128), BF)

    begin(sec_f)
    du(3, 6)
    store_ig = local(ig, ig_hbm.at[0], 6)
    store_ig.start()
    gather(sec_a, qa, rqa, x, s2a, 160)
    fives(s2a, ta)
    begin(thr_a[0])
    rta[c, 0] = ta[z, c]

    for sec, thr, q, rq, mine, s2, t, rt, i in (
            (sec_b, thr_b, qb, rqb, z, s2b, tb, rtb, y), (sec_c, thr_c, qc, rqc, y, s2c, tc, rtc, x)):
        gather(sec, q, rq, mine, s2, 288)
        rows36(s2, t)
        begin(thr[0])
        rt[c, 0] = t[i, c]

    gather(sec_f, qf, rqf, x, s2f, 288)

    @pl.when(c == 0)
    def _():
        rows36(s2f, tf)

    @pl.when(c == 1)
    def _():
        fives(s2f, tf)
        for n in range(4):
            for cc in range(2):
                tf[n, cc, 32:48] = jnp.zeros((16, 128), BF)

    begin(thr_f[0])
    rtf[c, 0] = tf[z, c]

    scale = 1.0 / (4 * 8192) ** 0.5

    def total(thr, rt):
        for cp in thr[1]:
            cp.wait_recv()
        return [(up32(rt[s, 0]) + up32(rt[s, 1]) + up32(rt[s, 2]) + up32(rt[s, 3])) * scale for s in range(2)]

    def put_proj(v, first):
        for b in range(4):
            po_ref[:, 128 * (first + b):128 * (first + b + 1)] = v[8 * b:8 * b + 5]

    low, high = total(thr_a, rta)
    put_proj(low, 0)
    put_proj(high, 4)
    for s, v in enumerate(total(thr_b, rtb)):
        fo_ref[:, 256 * s:256 * s + 128] = v[0:36]
    for s, v in enumerate(total(thr_c, rtc)):
        fo_ref[:, 256 * s + 128:256 * s + 256] = v[0:36]
    low, high = total(thr_f, rtf)
    fo_ref[:, 512:640] = low[0:36]
    put_proj(high, 8)

    @pl.when(has_next)
    def _():
        halo_up.wait_send()
        dz_up.wait_send()

    @pl.when(has_prev)
    def _():
        halo_dn.wait_send()
        dz_dn.wait_send()

    for cp in (sib_c, sib_u, sib_g, sib_d, sib_lo, sib_hi):
        cp.wait_send()
    def ring_left(part):
        for k in (0, 1):
            for w in range(3):
                steps[part][k][w].wait_send()

    ring_left("A")
    ring_left("B")
    ring_left("C")

    @pl.when(c == 0)
    def _():
        ring_left("F")

    @pl.when(c == 1)
    def _():
        ring_left("G")

    for cp in sec_a + sec_f + sec_b + sec_c + thr_a[0] + thr_f[0] + thr_b[0] + thr_c[0]:
        cp.wait_send()
    store_ig.wait()


def finish(*refs):
    ins, outs, held, sem = refs[:3], refs[3:6], refs[6:9], refs[9]
    come = [pltpu.make_async_copy(a, v, sem.at[i]) for i, (a, v) in enumerate(zip(ins, held))]
    go = [pltpu.make_async_copy(v, b, sem.at[3 + i]) for i, (v, b) in enumerate(zip(held, outs))]
    for cp in come:
        cp.start()
    for cp, then in zip(come, go):
        cp.wait()
        then.start()
    for cp in go:
        cp.wait()


def shards(inputs, cotangent, filter_weight, projection_weight):
    v = pltpu.VMEM
    anywhere = pl.BlockSpec(memory_space=pl.ANY)
    whole = pl.BlockSpec(memory_space=pltpu.VMEM)
    scratch = [
        v((T, C), BF), v((T, C), BF), v((2, C, T), BF), v((2 * T, C), BF), v((3 * C, H), BF), v((H, C), BF),
        v((2, D, H), BF), v((2, D, H), BF), v((T, H), F32), v((T, H), F32), v((T, H), BF),
        v((2, H, T), BF), v((2, T + 2 * D, H), BF), v((2, T + 2 * D, 384), BF),
        v((4, 640, 128), BF), v((4, 1152, 128), BF), v((4, 4, 288, 128), BF), v((4, 4, 2, 144, 128), BF),
        v((2, 320, 128), BF), v((2, 576, 128), BF), v((2, 2, 288, 128), BF), v((2, 2, 2, 144, 128), BF),
        v((2, 2, 320, 128), BF), v((2, 2, 576, 128), BF), v((2, 2, 2, 288, 128), BF), v((2, 2, 2, 2, 144, 128), BF),
        v((640, 128), F32), v((1152, 128), F32),
        v((4, 160, 128), BF), v((4, 288, 128), BF), v((4, 288, 128), BF), v((4, 288, 128), BF),
        v((3, 160, 128), BF), v((3, 288, 128), BF), v((3, 288, 128), BF), v((3, 288, 128), BF),
        v((168, 128), F32), v((304, 128), F32), v((304, 128), F32), v((304, 128), F32),
        v((4, 2, 32, 128), BF), v((4, 2, 48, 128), BF), v((4, 2, 48, 128), BF), v((4, 2, 48, 128), BF),
        v((2, 4, 32, 128), BF), v((2, 4, 48, 128), BF), v((2, 4, 48, 128), BF), v((2, 4, 48, 128), BF),
        v((T, C), BF),
        pltpu.SemaphoreType.DMA((8,)), pltpu.SemaphoreType.DMA((N_SEM,)), pltpu.SemaphoreType.DMA((N_SEM,)),
    ]
    shapes = (
        jax.ShapeDtypeStruct((1, T, C), BF),
        jax.ShapeDtypeStruct((36, H), F32),
        jax.ShapeDtypeStruct((5, C), F32),
    )
    results = pl.pallas_call(
        kernel,
        name="block_backward",
        out_shape=shapes,
        in_specs=[anywhere] * 4,
        out_specs=(anywhere, whole, whole),
        scratch_shapes=scratch,
        compiler_params=pltpu.CompilerParams(
            collective_id=0, has_side_effects=True, vmem_limit_bytes=56 * 2**20),
        cost_estimate=pl.CostEstimate(flops=5_600_000_000, bytes_accessed=12_000_000, transcendentals=1_000_000),
    )(inputs, cotangent, filter_weight, projection_weight)
    return pl.pallas_call(
        finish,
        name="hand_out",
        out_shape=shapes,
        in_specs=[anywhere] * 3,
        out_specs=[anywhere] * 3,
        scratch_shapes=[v(s.shape, s.dtype) for s in shapes] + [pltpu.SemaphoreType.DMA((6,))],
    )(*results)


def solution(mesh):
    in_specs = (P("grp", "seq", None), P("grp", "seq", None), P(), P())
    out_specs = (P("grp", "seq", None), P(("seq", "grp"), None), P(("seq", "grp"), None))
    return jax.shard_map(shards, mesh=mesh, in_specs=in_specs, out_specs=out_specs, check_vma=False)
```

```python
import jax
import jax.numpy as jnp
from jax import lax
from jax.experimental import pallas as pl
from jax.experimental.pallas import tpu as pltpu
from jax.sharding import PartitionSpec as P

MESH = pl.DeviceIdType.MESH
BF, F32 = jnp.bfloat16, jnp.float32
D = 64
T = 256
C = 1536
H = 640
COEFF = 0.7978845608028654
NT = (((1,), (1,)), ((), ()))

S_HALO = 0
S_DZ = 2
S_SIB = 4
S_P1 = 10
S_P2 = 46
S_P3 = 58
N_SEM = 90


def slot_b(xx, yy):
    if yy == (2 if xx < 2 else 1):
        return 0
    return {0: 1, 1: 2, 2: 2, 3: 3}[yy]


def row_c(yy, xp):
    return 144 * ((1, 1), (2, 0), (0, 0), (0, 1), (1, 0), (2, 1), (3, 0), (3, 1)).index((yy, xp))


def tanh_of(v):
    return jnp.tanh(COEFF * (v + 0.044715 * (v * v * v)))


def slope(v, t):
    return 0.5 * (1.0 + t) + 0.5 * v * (1.0 - t * t) * COEFF * (1.0 + 3.0 * 0.044715 * v * v)


def dot(a, b):
    return jnp.dot(a, b, preferred_element_type=F32)


def dot_nt(a, b):
    return lax.dot_general(a, b, NT, preferred_element_type=F32)


def up32(v):
    return v.astype(F32)


def kernel(x_hbm, cot_hbm, fw_hbm, pw_hbm, ig_hbm, fo_ref, po_ref,
           xv, ue, ut, cot, fw, pw, eo, ei, z_ref, dg_ref, g_ref, gt, dzx, dzc,
           pa, pf, pb, pc, rla, rlf, rlb, rlc, rfa, rff, rfb, rfc,
           sa, sf, sb, sc, qa, qf, qb, qc, rqa, rqf, rqb, rqc, s2a, s2f, s2b, s2c,
           ta, tf, tb, tc, rta, rtf, rtb, rtc, ig, lsem, ssem, rsem):
    seq, grp = lax.axis_index("seq"), lax.axis_index("grp")
    y, x, z, c = seq // 8, (seq // 2) % 4, (seq % 2) * 2 + grp // 2, grp % 2
    o = 1 - c

    def dev(xx, yy, zz, cc):
        return (yy * 8 + xx * 2 + zz // 2, (zz % 2) * 2 + cc)

    def at(axis, d, cc):
        xx = (x + d) % 4 if axis == "x" else x
        yy = (y + d) % 4 if axis == "y" else y
        zz = (z + d) % 4 if axis == "z" else z
        return dev(xx, yy, zz, cc)

    sibling = (seq, grp + 1 - 2 * c)
    pos = {"x": x, "y": y, "z": z}
    has_prev, has_next = seq > 0, seq < 31
    nxt, prv = (seq + 1, grp), (seq - 1, grp)

    def remote(src, dst, sem, device):
        return pltpu.make_async_remote_copy(
            src_ref=src, dst_ref=dst, send_sem=ssem.at[sem[0]], recv_sem=rsem.at[sem[1]],
            device_id=device, device_id_type=MESH)

    def local(src, dst, i):
        return pltpu.make_async_copy(src, dst, lsem.at[i])

    load_x = local(x_hbm.at[0], xv, 0)
    load_f = [local(fw_hbm.at[pl.ds(C * k, C)], fw.at[pl.ds(C * k, C)], 1 + k) for k in range(3)]
    load_c = local(cot_hbm.at[0], cot.at[pl.ds(0, T)], 4)
    load_p = local(pw_hbm, pw, 5)
    load_x.start()
    load_f[0].start()
    load_f[2].start()

    barrier = pltpu.get_barrier_semaphore()

    def greet(device):
        pl.semaphore_signal(barrier, inc=1, device_id=device, device_id_type=MESH)

    @pl.when(has_next)
    def _():
        greet(nxt)

    @pl.when(has_prev)
    def _():
        greet(prv)

    greet(sibling)
    for axis in ("x", "y", "z"):
        for d in (1, 2, 3):
            for cc in (0, 1):
                greet(at(axis, d, cc))

    def act(first, rows):
        v = up32(xv[pl.ds(first, rows)])
        ue[pl.ds(first, rows)] = (0.5 * v * (1.0 + tanh_of(v))).astype(BF)

    load_x.wait()
    for first in (192, 224, 0, 32):
        act(first, 32)
    load_f[0].wait()
    eo[0] = dot(ue[T - D:T], fw[0:C]).astype(BF)
    load_f[2].wait()
    load_f[1].start()
    load_c.start()
    load_p.start()
    eo[1] = dot(ue[0:D], fw[2 * C:3 * C]).astype(BF)

    pl.semaphore_wait(barrier, 19 + has_prev.astype(jnp.int32) + has_next.astype(jnp.int32))

    halo_up = remote(eo.at[0], ei.at[0], (S_HALO, S_HALO), nxt)
    halo_dn = remote(eo.at[1], ei.at[1], (S_HALO + 1, S_HALO + 1), prv)
    dz_up = remote(dzx.at[0, pl.ds(T, D)], dzx.at[0, pl.ds(0, D)], (S_DZ, S_DZ), nxt)
    dz_dn = remote(dzx.at[0, pl.ds(D, D)], dzx.at[0, pl.ds(D + T, D)], (S_DZ + 1, S_DZ + 1), prv)

    @pl.when(has_next)
    def _():
        halo_up.start()

    @pl.when(has_prev)
    def _():
        halo_dn.start()

    sib_c = remote(cot_hbm.at[0], cot.at[pl.ds(T, T)], (S_SIB, S_SIB), sibling)
    sib_u = remote(ut.at[0], ut.at[1], (S_SIB + 1, S_SIB + 1), sibling)
    sib_g = remote(gt.at[0], gt.at[1], (S_SIB + 2, S_SIB + 2), sibling)

    def sib_dz(first, rows, sem):
        return remote(dzx.at[0, pl.ds(first, rows)], dzx.at[1, pl.ds(first, rows)], (sem, sem), sibling)

    sib_d = sib_dz(D, T, S_SIB + 3)
    sib_lo = sib_dz(0, D, S_SIB + 4)
    sib_hi = sib_dz(D + T, D, S_SIB + 5)
    sib_c.start()

    @pl.loop(0, 4)
    def _(i):
        act(pl.multiple_of(D + i * 32, 32), 32)

    ut[0, :, 0:128] = ue[0:128].T
    ut[0, :, 128:256] = ue[128:256].T
    sib_u.start()

    load_f[1].wait()
    z_ref[...] = dot(ue[...], fw[C:2 * C])
    z_ref[64:256] += dot(ue[0:192], fw[0:C])
    z_ref[0:192] += dot(ue[64:256], fw[2 * C:3 * C])
    load_c.wait()
    load_p.wait()
    dg_ref[...] = dot_nt(cot[0:T], pw[...])

    def inner(first):
        rows = pl.ds(first, 32)
        v = z_ref[rows]
        t = tanh_of(v)
        g_ref[rows] = (0.5 * v * (1.0 + t)).astype(BF)
        dzx[0, pl.ds(D + first, 32)] = (dg_ref[rows] * slope(v, t)).astype(BF)

    for first in (64, 96, 128, 160):
        inner(first)

    @pl.when(has_prev)
    def _():
        halo_up.wait_recv()
        z_ref[0:64] += up32(ei[0])

    @pl.when(has_next)
    def _():
        halo_dn.wait_recv()
        z_ref[192:256] += up32(ei[1])

    for first in (0, 32, 192, 224):
        inner(first)

    @pl.when(has_next)
    def _():
        dz_up.start()

    @pl.when(has_prev)
    def _():
        dz_dn.start()

    gt[0] = g_ref[...].T
    sib_g.start()
    sib_d.start()

    def flat(p, first, rows):
        return lambda j, h: p.at[j, pl.ds(first + rows * h, rows)]

    def cut(r, first, rows):
        return r.at[..., pl.ds(first, rows), :]

    rings = {
        "A": ("y", flat(pa, 0, 320), rla, rfa, S_P1),
        "F": ("y", flat(pf, 0, 576), rlf, rff, S_P1 + 6),
        "G": ("y", flat(pf, 0, 320), cut(rlf, 0, 320), cut(rff, 0, 320), S_P1 + 6),
        "B0": ("x", flat(pb, 0, 144), cut(rlb, 0, 144), cut(rfb, 0, 144), S_P1 + 12),
        "B1": ("x", flat(pb, 288, 432), cut(rlb, 144, 432), cut(rfb, 144, 432), S_P1 + 18),
        "C0": ("z", flat(pc, 0, 144), cut(rlc, 0, 144), cut(rfc, 0, 144), S_P1 + 24),
        "C1": ("z", flat(pc, 288, 432), cut(rlc, 144, 432), cut(rfc, 144, 432), S_P1 + 30),
    }

    def ring(part):
        axis, chunk, rl, rf, sem = rings[part]
        i = pos[axis]
        up, far, dn = (i + 1) % 4, (i + 2) % 4, (i + 3) % 4
        out = []
        for k, (near, h, to) in enumerate(((up, 0, 1), (dn, 1, 3))):
            who = at(axis, to, c)
            s = sem + 3 * k
            out.append((
                remote(chunk(far, h), rl.at[k], (s, s), who),
                remote(chunk(near, 1 - h), rf.at[k, 0], (s + 1, s + 1), who),
                remote(chunk(near, h), rf.at[k, 1], (s + 2, s + 2), who),
                chunk(near, h), rl.at[k]))
        return out

    steps = {part: ring(part) for part in rings}

    def ring_start(part):
        for which in (0, 1):
            for k in (0, 1):
                steps[part][k][which].start()

    def ring_relay(part):
        for k in (0, 1):
            first, _, second, mine, came = steps[part][k]
            first.wait_recv()
            mine[...] = (up32(mine[...]) + up32(came[...])).astype(BF)
            second.start()

    def ring_end(part):
        for k in (0, 1):
            steps[part][k][1].wait_recv()
            steps[part][k][2].wait_recv()

    def proj(to, first, n):
        cols = pl.ds(pl.multiple_of(first, 256), 256)
        acc = dot(gt[0], cot[0:T, cols]) + dot(gt[1], cot[T:2 * T, cols])
        for j in range(4):
            for b in range(2):
                to[j, 320 * n + 160 * b:320 * n + 160 * (b + 1)] = (
                    acc[160 * j:160 * (j + 1), 128 * b:128 * (b + 1)].astype(BF))

    sib_c.wait_recv()
    sib_g.wait_recv()
    for n in range(2):
        proj(pa, 512 * c + 256 * n, n)
    ring_start("A")

    @pl.when(c == 1)
    def _():
        for n in range(2):
            proj(pf, 1024 + 256 * n, n)
        ring_start("G")

    def columns(s, first, rows):
        r = pl.ds(first, rows)
        dzc[s, r, 0:256] = dzx[s, r, pl.ds(pl.multiple_of(256 * c, 256), 256)]
        dzc[s, r, 256:384] = dzx[s, r, 512:640]

    def rhs(tap, lo, hi):
        r = pl.ds(D * (2 - tap), T)
        return jnp.concatenate([dzc[0, r, lo:hi], dzc[1, r, lo:hi]], axis=0)

    def rows_of(first, rows, lo, hi):
        out = []
        last = first + rows
        while first < last:
            tap = first // C
            stop = min(last, C * (tap + 1))
            r = slice(first - C * tap, stop - C * tap)
            left = jnp.concatenate([ut[0, r], ut[1, r]], axis=1)
            out.append(dot(left, rhs(tap, lo, hi)))
            first = stop
        return out[0] if len(out) == 1 else jnp.concatenate(out, axis=0)

    def filt(n):
        yy, xp = n // 2, n % 2
        acc = rows_of(576 * n, 576, 0, 256)
        for b in range(2):
            first = 288 * slot_b(2 * xp + b, yy)
            pb[2 * xp + b, first:first + 288] = acc[288 * b:288 * (b + 1), 0:128].astype(BF)
        first = row_c(yy, xp)
        for zz in range(4):
            pc[zz, first:first + 144] = jnp.concatenate(
                [acc[72 * zz:72 * zz + 72, 128:256], acc[288 + 72 * zz:360 + 72 * zz, 128:256]],
                axis=0).astype(BF)

    columns(0, D, T)
    sib_u.wait_recv()
    sib_d.wait_recv()
    columns(1, D, T)
    filt(3)
    filt(4)
    ring_start("B0")
    @pl.when(has_prev)
    def _():
        dz_up.wait_recv()

    @pl.when(jnp.logical_not(has_prev))
    def _():
        dzx[0, 0:D] = jnp.zeros((D, H), BF)

    sib_lo.start()

    @pl.when(has_next)
    def _():
        dz_dn.wait_recv()

    @pl.when(jnp.logical_not(has_next))
    def _():
        dzx[0, D + T:D + T + D] = jnp.zeros((D, H), BF)

    sib_hi.start()
    columns(0, 0, D)
    columns(0, D + T, D)
    ring_start("C0")
    ring_relay("A")
    ring_relay("B0")
    sib_lo.wait_recv()
    sib_hi.wait_recv()
    columns(1, 0, D)
    columns(1, D + T, D)
    for n in (0, 1, 2, 5, 6, 7):
        filt(n)
    ring_start("B1")
    ring_start("C1")
    ring_relay("C0")

    @pl.when(c == 0)
    def _():
        for n in range(8):
            pf[n // 2, 576 * (n % 2):576 * (n % 2 + 1)] = rows_of(576 * n, 576, 256, 384).astype(BF)
        ring_start("F")

    def du(lo, hi):
        @pl.loop(lo, hi)
        def _(n):
            cols = pl.ds(pl.multiple_of(256 * n, 256), 256)
            acc = jnp.zeros((T, 256), F32)
            for k in range(3):
                rows = pl.ds(pl.multiple_of(C * k + 256 * n, 256), 256)
                acc += dot_nt(dzx[0, D * (2 - k):D * (2 - k) + T], fw[rows])
            v = up32(xv[:, cols])
            ig[:, cols] = (up32(cot[0:T, cols]) + acc * slope(v, tanh_of(v))).astype(BF)

    def second(axis, q, rq, sem):
        return [remote(q.at[(pos[axis] + d) % 4], rq.at[d - 1], (sem + d - 1, sem + d - 1), at(axis, d, c))
                for d in (1, 2, 3)]

    sec_a = second("x", qa, rqa, S_P2)
    sec_f = second("x", qf, rqf, S_P2 + 3)
    sec_g = [remote(qf.at[(x + d) % 4, pl.ds(0, 160)], rqf.at[d - 1, pl.ds(0, 160)],
                    (S_P2 + 2 + d, S_P2 + 2 + d), at("x", d, c)) for d in (1, 2, 3)]
    sec_b = second("z", qb, rqb, S_P2 + 6)
    sec_c = second("y", qc, rqc, S_P2 + 9)

    def third(axis, t, rt, sem):
        i = pos[axis]
        out = []
        for d in (2, 1, 3):
            for cc in (0, 1):
                out.append(remote(t.at[(i + d) % 4, cc], rt.at[c, d],
                                  (sem + 4 * cc + d, sem + 4 * c + d), at(axis, d, cc)))
        out.append(remote(t.at[i, o], rt.at[c, 0], (sem + 4 * o, sem + 4 * c), sibling))
        wait = []
        for s in (0, 1):
            for d in (1, 2, 3):
                wait.append(remote(t.at[0, 0], rt.at[s, d], (sem + 4 * s + d, sem + 4 * s + d), sibling))
        wait.append(remote(t.at[0, 0], rt.at[o, 0], (sem + 4 * o, sem + 4 * o), sibling))
        return out, wait

    thr_a = third("z", ta, rta, S_P3)
    thr_f = third("z", tf, rtf, S_P3 + 8)
    thr_b = third("y", tb, rtb, S_P3 + 16)
    thr_c = third("x", tc, rtc, S_P3 + 24)

    def begin(copies):
        for cp in copies:
            cp.start()

    def pairs(q, s):
        for p in range(2):
            for xx in range(4):
                lo = 320 * p + 40 * xx
                q[xx, 80 * p:80 * (p + 1)] = jnp.concatenate(
                    [s[lo:lo + 40], s[lo + 160:lo + 200]], axis=0).astype(BF)

    def gather(sec, q, rq, mine, s2, rows):
        for cp in sec:
            cp.wait_recv()
        r = pl.ds(0, rows)
        s2[r] = up32(q[mine, r]) + up32(rq[0, r]) + up32(rq[1, r]) + up32(rq[2, r])

    def rows36(s2, t, owners=(0, 1, 2, 3)):
        for n, owner in enumerate(owners):
            for cc in range(2):
                lo = 72 * n + 36 * cc
                t[owner, cc] = s2[lo:lo + 48].astype(BF)

    def fives(s2, t):
        for p in range(2):
            for n in range(4):
                for cc in range(2):
                    lo = 80 * p + 10 * n + 5 * cc
                    t[n, cc, 16 * p:16 * (p + 1)] = jnp.concatenate(
                        [s2[lo:lo + 8], s2[lo + 40:lo + 48]], axis=0).astype(BF)

    @pl.when(c == 1)
    def _():
        ring_relay("G")

    du(0, 3)
    ring_relay("B1")
    ring_relay("C1")

    @pl.when(c == 0)
    def _():
        ring_relay("F")
    ring_end("A")
    for h in range(2):
        sa[320 * h:320 * (h + 1)] = up32(pa[y, 320 * h:320 * (h + 1)]) + up32(rfa[0, 1 - h]) + up32(rfa[1, h])
    pairs(qa, sa)
    begin(sec_a)


    s2a[160:168] = jnp.zeros((8, 128), F32)
    s2f[288:304] = jnp.zeros((16, 128), F32)
    s2b[288:304] = jnp.zeros((16, 128), F32)
    s2c[288:304] = jnp.zeros((16, 128), F32)
    def sum_bc(p, i, rf, to):
        for first, off, rows in ((0, 0, 144), (288, 144, 432)):
            for h in range(2):
                r, f = pl.ds(first + rows * h, rows), pl.ds(off, rows)
                to[r] = up32(p[i, r]) + up32(rf[0, 1 - h, f]) + up32(rf[1, h, f])

    ring_end("B0")
    ring_end("B1")
    sum_bc(pb, x, rfb, sb)
    for h in range(2):
        for zz in range(4):
            lo = 576 * h + 72 * zz
            qb[zz, 144 * h:144 * (h + 1)] = jnp.concatenate(
                [sb[lo:lo + 72], sb[lo + 288:lo + 360]], axis=0).astype(BF)
    begin(sec_b)

    ring_end("C0")
    ring_end("C1")
    sum_bc(pc, z, rfc, sc)
    for yy in range(4):
        for xp in range(2):
            lo = row_c(yy, xp)
            qc[yy, 144 * xp:144 * (xp + 1)] = sc[lo:lo + 144].astype(BF)
    begin(sec_c)

    def sum_f(rows):
        for h in range(2):
            r = pl.ds(rows * h, rows)
            sf[r] = up32(pf[y, r]) + up32(rff[0, 1 - h, 0:rows]) + up32(rff[1, h, 0:rows])

    @pl.when(c == 0)
    def _():
        ring_end("F")
        sum_f(576)
        for xx in range(4):
            qf[xx] = sf[288 * xx:288 * (xx + 1)].astype(BF)
        begin(sec_f)

    @pl.when(c == 1)
    def _():
        ring_end("G")
        sum_f(320)
        pairs(qf, sf)
        begin(sec_g)

    du(3, 6)
    store_ig = local(ig, ig_hbm.at[0], 6)
    store_ig.start()
    gather(sec_a, qa, rqa, x, s2a, 160)
    fives(s2a, ta)
    begin(thr_a[0])
    rta[c, 0] = ta[z, c]

    mid = jnp.where(x < 2, 1, 0)
    for sec, thr, q, rq, mine, s2, t, rt, i, owners in (
            (sec_b, thr_b, qb, rqb, z, s2b, tb, rtb, y, (1 + mid, 0, 2 - mid, 3)),
            (sec_c, thr_c, qc, rqc, y, s2c, tc, rtc, x, (0, 1, 2, 3))):
        gather(sec, q, rq, mine, s2, 288)
        rows36(s2, t, owners)
        begin(thr[0])
        rt[c, 0] = t[i, c]

    @pl.when(c == 0)
    def _():
        gather(sec_f, qf, rqf, x, s2f, 288)
        rows36(s2f, tf)

    @pl.when(c == 1)
    def _():
        gather(sec_g, qf, rqf, x, s2f, 160)
        s2f[160:168] = jnp.zeros((8, 128), F32)
        fives(s2f, tf)
        for n in range(4):
            for cc in range(2):
                tf[n, cc, 32:48] = jnp.zeros((16, 128), BF)

    begin(thr_f[0])
    rtf[c, 0] = tf[z, c]

    scale = 1.0 / (4 * 8192) ** 0.5

    def total(thr, rt):
        for cp in thr[1]:
            cp.wait_recv()
        return [(up32(rt[s, 0]) + up32(rt[s, 1]) + up32(rt[s, 2]) + up32(rt[s, 3])) * scale for s in range(2)]

    def put_proj(v, first):
        for b in range(4):
            po_ref[:, 128 * (first + b):128 * (first + b + 1)] = v[8 * b:8 * b + 5]

    low, high = total(thr_a, rta)
    put_proj(low, 0)
    put_proj(high, 4)
    for s, v in enumerate(total(thr_b, rtb)):
        fo_ref[:, 256 * s:256 * s + 128] = v[0:36]
    for s, v in enumerate(total(thr_c, rtc)):
        fo_ref[:, 256 * s + 128:256 * s + 256] = v[0:36]
    low, high = total(thr_f, rtf)
    fo_ref[:, 512:640] = low[0:36]
    put_proj(high, 8)

    @pl.when(has_next)
    def _():
        halo_up.wait_send()
        dz_up.wait_send()

    @pl.when(has_prev)
    def _():
        halo_dn.wait_send()
        dz_dn.wait_send()

    for cp in (sib_c, sib_u, sib_g, sib_d, sib_lo, sib_hi):
        cp.wait_send()
    def ring_left(part):
        for k in (0, 1):
            for w in range(3):
                steps[part][k][w].wait_send()

    ring_left("A")
    ring_left("B0")
    ring_left("B1")
    ring_left("C0")
    ring_left("C1")

    @pl.when(c == 0)
    def _():
        ring_left("F")
        for cp in sec_f:
            cp.wait_send()

    @pl.when(c == 1)
    def _():
        ring_left("G")
        for cp in sec_g:
            cp.wait_send()

    for cp in sec_a + sec_b + sec_c + thr_a[0] + thr_f[0] + thr_b[0] + thr_c[0]:
        cp.wait_send()
    store_ig.wait()


def finish(*refs):
    ins, outs, held, sem = refs[:3], refs[3:6], refs[6:9], refs[9]
    come = [pltpu.make_async_copy(a, v, sem.at[i]) for i, (a, v) in enumerate(zip(ins, held))]
    go = [pltpu.make_async_copy(v, b, sem.at[3 + i]) for i, (v, b) in enumerate(zip(held, outs))]
    for cp in come:
        cp.start()
    for cp, then in zip(come, go):
        cp.wait()
        then.start()
    for cp in go:
        cp.wait()


def shards(inputs, cotangent, filter_weight, projection_weight):
    v = pltpu.VMEM
    anywhere = pl.BlockSpec(memory_space=pl.ANY)
    whole = pl.BlockSpec(memory_space=pltpu.VMEM)
    scratch = [
        v((T, C), BF), v((T, C), BF), v((2, C, T), BF), v((2 * T, C), BF), v((3 * C, H), BF), v((H, C), BF),
        v((2, D, H), BF), v((2, D, H), BF), v((T, H), F32), v((T, H), F32), v((T, H), BF),
        v((2, H, T), BF), v((2, T + 2 * D, H), BF), v((2, T + 2 * D, 384), BF),
        v((4, 640, 128), BF), v((4, 1152, 128), BF), v((4, 1152, 128), BF), v((4, 1152, 128), BF),
        v((2, 320, 128), BF), v((2, 576, 128), BF), v((2, 576, 128), BF), v((2, 576, 128), BF),
        v((2, 2, 320, 128), BF), v((2, 2, 576, 128), BF), v((2, 2, 576, 128), BF), v((2, 2, 576, 128), BF),
        v((640, 128), F32), v((1152, 128), F32), v((1152, 128), F32), v((1152, 128), F32),
        v((4, 160, 128), BF), v((4, 288, 128), BF), v((4, 288, 128), BF), v((4, 288, 128), BF),
        v((3, 160, 128), BF), v((3, 288, 128), BF), v((3, 288, 128), BF), v((3, 288, 128), BF),
        v((168, 128), F32), v((304, 128), F32), v((304, 128), F32), v((304, 128), F32),
        v((4, 2, 32, 128), BF), v((4, 2, 48, 128), BF), v((4, 2, 48, 128), BF), v((4, 2, 48, 128), BF),
        v((2, 4, 32, 128), BF), v((2, 4, 48, 128), BF), v((2, 4, 48, 128), BF), v((2, 4, 48, 128), BF),
        v((T, C), BF),
        pltpu.SemaphoreType.DMA((8,)), pltpu.SemaphoreType.DMA((N_SEM,)), pltpu.SemaphoreType.DMA((N_SEM,)),
    ]
    shapes = (
        jax.ShapeDtypeStruct((1, T, C), BF),
        jax.ShapeDtypeStruct((36, H), F32),
        jax.ShapeDtypeStruct((5, C), F32),
    )
    results = pl.pallas_call(
        kernel,
        name="block_backward",
        out_shape=shapes,
        in_specs=[anywhere] * 4,
        out_specs=(anywhere, whole, whole),
        scratch_shapes=scratch,
        compiler_params=pltpu.CompilerParams(
            collective_id=0, has_side_effects=True, vmem_limit_bytes=56 * 2**20),
        cost_estimate=pl.CostEstimate(flops=5_600_000_000, bytes_accessed=12_000_000, transcendentals=1_000_000),
    )(inputs, cotangent, filter_weight, projection_weight)
    return pl.pallas_call(
        finish,
        name="hand_out",
        out_shape=shapes,
        in_specs=[anywhere] * 3,
        out_specs=[anywhere] * 3,
        scratch_shapes=[v(s.shape, s.dtype) for s in shapes] + [pltpu.SemaphoreType.DMA((6,))],
    )(*results)


def solution(mesh):
    in_specs = (P("grp", "seq", None), P("grp", "seq", None), P(), P())
    out_specs = (P("grp", "seq", None), P(("seq", "grp"), None), P(("seq", "grp"), None))
    return jax.shard_map(shards, mesh=mesh, in_specs=in_specs, out_specs=out_specs, check_vma=False)
```

```python
import jax
import jax.numpy as jnp
from jax import lax
from jax.experimental import pallas as pl
from jax.experimental.pallas import tpu as pltpu
from jax.sharding import PartitionSpec as P

MESH = pl.DeviceIdType.MESH
BF, F32 = jnp.bfloat16, jnp.float32
D = 64
T = 256
C = 1536
H = 640
COEFF = 0.7978845608028654
NT = (((1,), (1,)), ((), ()))

S_HALO = 0
S_DZ = 2
S_SIB = 4
S_P1 = 10
S_P2 = 64
S_P3 = 76
N_SEM = 108


PIECES = ((0, 0, 144), (288, 144, 224), (736, 368, 208))
PIECES_F = ((0, 0, 288), (576, 288, 288))


def slot_b(xx, yy):
    if yy == (2 if xx < 2 else 1):
        return 0
    return {0: 1, 1: 2, 2: 2, 3: 3}[yy]


def row_c(yy, xp):
    return 144 * ((1, 1), (2, 0), (0, 0), (0, 1), (1, 0), (2, 1), (3, 0), (3, 1)).index((yy, xp))


def tanh_of(v):
    return jnp.tanh(COEFF * (v + 0.044715 * (v * v * v)))


def slope(v, t):
    return 0.5 * (1.0 + t) + 0.5 * v * (1.0 - t * t) * COEFF * (1.0 + 3.0 * 0.044715 * v * v)


def dot(a, b):
    return jnp.dot(a, b, preferred_element_type=F32)


def dot_nt(a, b):
    return lax.dot_general(a, b, NT, preferred_element_type=F32)


def up32(v):
    return v.astype(F32)


def kernel(x_hbm, cot_hbm, fw_hbm, pw_hbm, ig_hbm, fo_ref, po_ref,
           xv, ue, ut, cot, fw, pw, eo, ei, z_ref, dg_ref, g_ref, gt, dzx, dzc,
           pa, pf, pb, pc, rla, rlf, rlb, rlc, rfa, rff, rfb, rfc,
           sa, sf, sb, sc, qa, qf, qb, qc, rqa, rqf, rqb, rqc, s2a, s2f, s2b, s2c,
           ta, tf, tb, tc, rta, rtf, rtb, rtc, ig, lsem, ssem, rsem):
    seq, grp = lax.axis_index("seq"), lax.axis_index("grp")
    y, x, z, c = seq // 8, (seq // 2) % 4, (seq % 2) * 2 + grp // 2, grp % 2
    o = 1 - c

    def dev(xx, yy, zz, cc):
        return (yy * 8 + xx * 2 + zz // 2, (zz % 2) * 2 + cc)

    def at(axis, d, cc):
        xx = (x + d) % 4 if axis == "x" else x
        yy = (y + d) % 4 if axis == "y" else y
        zz = (z + d) % 4 if axis == "z" else z
        return dev(xx, yy, zz, cc)

    sibling = (seq, grp + 1 - 2 * c)
    pos = {"x": x, "y": y, "z": z}
    has_prev, has_next = seq > 0, seq < 31
    nxt, prv = (seq + 1, grp), (seq - 1, grp)

    def remote(src, dst, sem, device):
        return pltpu.make_async_remote_copy(
            src_ref=src, dst_ref=dst, send_sem=ssem.at[sem[0]], recv_sem=rsem.at[sem[1]],
            device_id=device, device_id_type=MESH)

    def local(src, dst, i):
        return pltpu.make_async_copy(src, dst, lsem.at[i])

    load_x = local(x_hbm.at[0], xv, 0)
    load_f = [local(fw_hbm.at[pl.ds(C * k, C)], fw.at[pl.ds(C * k, C)], 1 + k) for k in range(3)]
    load_c = local(cot_hbm.at[0], cot.at[pl.ds(0, T)], 4)
    load_p = local(pw_hbm, pw, 5)
    load_x.start()
    load_f[0].start()
    load_f[2].start()

    barrier = pltpu.get_barrier_semaphore()

    def greet(device):
        pl.semaphore_signal(barrier, inc=1, device_id=device, device_id_type=MESH)

    @pl.when(has_next)
    def _():
        greet(nxt)

    @pl.when(has_prev)
    def _():
        greet(prv)

    greet(sibling)
    for axis in ("x", "y", "z"):
        for d in (1, 2, 3):
            for cc in (0, 1):
                greet(at(axis, d, cc))

    def act(first, rows):
        v = up32(xv[pl.ds(first, rows)])
        ue[pl.ds(first, rows)] = (0.5 * v * (1.0 + tanh_of(v))).astype(BF)

    load_x.wait()
    for first in (192, 224, 0, 32):
        act(first, 32)
    pl.semaphore_wait(barrier, 19 + has_prev.astype(jnp.int32) + has_next.astype(jnp.int32))
    halo_up = remote(eo.at[0], ei.at[0], (S_HALO, S_HALO), nxt)
    halo_dn = remote(eo.at[1], ei.at[1], (S_HALO + 1, S_HALO + 1), prv)
    dz_up = remote(dzx.at[0, pl.ds(T, D)], dzx.at[0, pl.ds(0, D)], (S_DZ, S_DZ), nxt)
    dz_dn = remote(dzx.at[0, pl.ds(D, D)], dzx.at[0, pl.ds(D + T, D)], (S_DZ + 1, S_DZ + 1), prv)

    load_f[0].wait()
    eo[0] = dot(ue[T - D:T], fw[0:C]).astype(BF)

    @pl.when(has_next)
    def _():
        halo_up.start()

    load_f[2].wait()
    load_f[1].start()
    load_c.start()
    load_p.start()
    eo[1] = dot(ue[0:D], fw[2 * C:3 * C]).astype(BF)

    @pl.when(has_prev)
    def _():
        halo_dn.start()

    sib_c = remote(cot_hbm.at[0], cot.at[pl.ds(T, T)], (S_SIB, S_SIB), sibling)
    sib_u = remote(ut.at[0], ut.at[1], (S_SIB + 1, S_SIB + 1), sibling)
    sib_g = remote(gt.at[0], gt.at[1], (S_SIB + 2, S_SIB + 2), sibling)

    def sib_dz(first, rows, sem):
        return remote(dzx.at[0, pl.ds(first, rows)], dzx.at[1, pl.ds(first, rows)], (sem, sem), sibling)

    sib_d = sib_dz(D, T, S_SIB + 3)
    sib_lo = sib_dz(0, D, S_SIB + 4)
    sib_hi = sib_dz(D + T, D, S_SIB + 5)
    sib_c.start()

    @pl.loop(0, 4)
    def _(i):
        act(pl.multiple_of(D + i * 32, 32), 32)

    ut[0, :, 0:128] = ue[0:128].T
    ut[0, :, 128:256] = ue[128:256].T
    sib_u.start()

    load_f[1].wait()
    z_ref[...] = dot(ue[...], fw[C:2 * C])
    z_ref[64:256] += dot(ue[0:192], fw[0:C])
    z_ref[0:192] += dot(ue[64:256], fw[2 * C:3 * C])
    load_c.wait()
    load_p.wait()
    dg_ref[...] = dot_nt(cot[0:T], pw[...])

    def inner(first):
        rows = pl.ds(first, 32)
        v = z_ref[rows]
        t = tanh_of(v)
        g_ref[rows] = (0.5 * v * (1.0 + t)).astype(BF)
        dzx[0, pl.ds(D + first, 32)] = (dg_ref[rows] * slope(v, t)).astype(BF)

    for first in (64, 96, 128, 160):
        inner(first)

    @pl.when(has_prev)
    def _():
        halo_up.wait_recv()
        z_ref[0:64] += up32(ei[0])

    inner(0)
    inner(32)

    @pl.when(has_prev)
    def _():
        dz_dn.start()

    @pl.when(has_next)
    def _():
        halo_dn.wait_recv()
        z_ref[192:256] += up32(ei[1])

    inner(192)
    inner(224)

    @pl.when(has_next)
    def _():
        dz_up.start()

    gt[0] = g_ref[...].T
    sib_g.start()
    sib_d.start()

    def flat(p, first, rows):
        return lambda j, h: p.at[j, pl.ds(first + rows * h, rows)]

    def cut(r, first, rows):
        return r.at[..., pl.ds(first, rows), :]

    rings = {
        "A": ("y", flat(pa, 0, 320), rla, rfa, S_P1),
        "G": ("y", flat(pf, 0, 320), cut(rlf, 0, 320), cut(rff, 0, 320), S_P1 + 6),
    }
    for n, (first, off, rows) in enumerate(PIECES_F):
        rings[f"F{n}"] = ("y", flat(pf, first, rows), cut(rlf, off, rows), cut(rff, off, rows), S_P1 + 6 + 6 * n)
    for n, (first, off, rows) in enumerate(PIECES):
        rings[f"B{n}"] = ("x", flat(pb, first, rows), cut(rlb, off, rows), cut(rfb, off, rows), S_P1 + 18 + 6 * n)
        rings[f"C{n}"] = ("z", flat(pc, first, rows), cut(rlc, off, rows), cut(rfc, off, rows), S_P1 + 36 + 6 * n)

    def ring(part):
        axis, chunk, rl, rf, sem = rings[part]
        i = pos[axis]
        up, far, dn = (i + 1) % 4, (i + 2) % 4, (i + 3) % 4
        out = []
        for k, (near, h, to) in enumerate(((up, 0, 1), (dn, 1, 3))):
            who = at(axis, to, c)
            s = sem + 3 * k
            out.append((
                remote(chunk(far, h), rl.at[k], (s, s), who),
                remote(chunk(near, 1 - h), rf.at[k, 0], (s + 1, s + 1), who),
                remote(chunk(near, h), rf.at[k, 1], (s + 2, s + 2), who),
                chunk(near, h), rl.at[k]))
        return out

    steps = {part: ring(part) for part in rings}

    def ring_far(part):
        for k in (0, 1):
            steps[part][k][0].start()

    def ring_near(part):
        for k in (0, 1):
            steps[part][k][1].start()

    def ring_start(part):
        ring_far(part)
        ring_near(part)

    def ring_relay(part):
        for k in (0, 1):
            first, _, second, mine, came = steps[part][k]
            first.wait_recv()
            mine[...] = (up32(mine[...]) + up32(came[...])).astype(BF)
            second.start()

    def ring_end(part):
        for k in (0, 1):
            steps[part][k][1].wait_recv()
            steps[part][k][2].wait_recv()

    def proj(to, first, n):
        cols = pl.ds(pl.multiple_of(first, 256), 256)
        acc = dot(gt[0], cot[0:T, cols]) + dot(gt[1], cot[T:2 * T, cols])
        for j in range(4):
            for b in range(2):
                to[j, 320 * n + 160 * b:320 * n + 160 * (b + 1)] = (
                    acc[160 * j:160 * (j + 1), 128 * b:128 * (b + 1)].astype(BF))

    sib_c.wait_recv()
    sib_g.wait_recv()
    for n in range(2):
        proj(pa, 512 * c + 256 * n, n)
    ring_start("A")

    @pl.when(c == 1)
    def _():
        for n in range(2):
            proj(pf, 1024 + 256 * n, n)
        ring_start("G")

    def columns(s, first, rows):
        r = pl.ds(first, rows)
        dzc[s, r, 0:256] = dzx[s, r, pl.ds(pl.multiple_of(256 * c, 256), 256)]
        dzc[s, r, 256:384] = dzx[s, r, 512:640]

    def rhs(tap, lo, hi):
        r = pl.ds(D * (2 - tap), T)
        return jnp.concatenate([dzc[0, r, lo:hi], dzc[1, r, lo:hi]], axis=0)

    def rows_of(first, rows, lo, hi):
        out = []
        last = first + rows
        while first < last:
            tap = first // C
            stop = min(last, C * (tap + 1))
            r = slice(first - C * tap, stop - C * tap)
            left = jnp.concatenate([ut[0, r], ut[1, r]], axis=1)
            out.append(dot(left, rhs(tap, lo, hi)))
            first = stop
        return out[0] if len(out) == 1 else jnp.concatenate(out, axis=0)

    def filt(n):
        yy, xp = n // 2, n % 2
        acc = rows_of(576 * n, 576, 0, 256)
        for b in range(2):
            first = 288 * slot_b(2 * xp + b, yy)
            pb[2 * xp + b, first:first + 288] = acc[288 * b:288 * (b + 1), 0:128].astype(BF)
        first = row_c(yy, xp)
        for zz in range(4):
            pc[zz, first:first + 144] = jnp.concatenate(
                [acc[72 * zz:72 * zz + 72, 128:256], acc[288 + 72 * zz:360 + 72 * zz, 128:256]],
                axis=0).astype(BF)

    columns(0, D, T)
    sib_u.wait_recv()
    sib_d.wait_recv()
    columns(1, D, T)
    filt(3)
    filt(4)
    ring_start("B0")
    @pl.when(has_prev)
    def _():
        dz_up.wait_recv()

    @pl.when(jnp.logical_not(has_prev))
    def _():
        dzx[0, 0:D] = jnp.zeros((D, H), BF)

    sib_lo.start()

    @pl.when(has_next)
    def _():
        dz_dn.wait_recv()

    @pl.when(jnp.logical_not(has_next))
    def _():
        dzx[0, D + T:D + T + D] = jnp.zeros((D, H), BF)

    sib_hi.start()
    columns(0, 0, D)
    columns(0, D + T, D)
    ring_start("C0")
    ring_relay("A")
    ring_relay("B0")
    sib_lo.wait_recv()
    sib_hi.wait_recv()
    columns(1, 0, D)
    columns(1, D + T, D)
    for n in (0, 1, 2, 5, 6, 7):
        filt(n)
    late = ("B1", "C1", "B2", "C2")
    for part in late:
        ring_far(part)
    ring_relay("C0")

    @pl.when(c == 0)
    def _():
        for n in range(8):
            pf[n // 2, 576 * (n % 2):576 * (n % 2 + 1)] = rows_of(576 * n, 576, 256, 384).astype(BF)
        ring_far("F0")
        ring_far("F1")

    def du(lo, hi):
        @pl.loop(lo, hi)
        def _(n):
            cols = pl.ds(pl.multiple_of(256 * n, 256), 256)
            acc = jnp.zeros((T, 256), F32)
            for k in range(3):
                rows = pl.ds(pl.multiple_of(C * k + 256 * n, 256), 256)
                acc += dot_nt(dzx[0, D * (2 - k):D * (2 - k) + T], fw[rows])
            v = up32(xv[:, cols])
            ig[:, cols] = (up32(cot[0:T, cols]) + acc * slope(v, tanh_of(v))).astype(BF)

    def second(axis, q, rq, sem):
        return [remote(q.at[(pos[axis] + d) % 4], rq.at[d - 1], (sem + d - 1, sem + d - 1), at(axis, d, c))
                for d in (1, 2, 3)]

    sec_a = second("x", qa, rqa, S_P2)
    sec_f = second("x", qf, rqf, S_P2 + 3)
    sec_g = [remote(qf.at[(x + d) % 4, pl.ds(0, 160)], rqf.at[d - 1, pl.ds(0, 160)],
                    (S_P2 + 2 + d, S_P2 + 2 + d), at("x", d, c)) for d in (1, 2, 3)]
    sec_b = second("z", qb, rqb, S_P2 + 6)
    sec_c = second("y", qc, rqc, S_P2 + 9)

    def third(axis, t, rt, sem):
        i = pos[axis]
        out = []
        for d in (2, 1, 3):
            for cc in (0, 1):
                out.append(remote(t.at[(i + d) % 4, cc], rt.at[c, d],
                                  (sem + 4 * cc + d, sem + 4 * c + d), at(axis, d, cc)))
        out.append(remote(t.at[i, o], rt.at[c, 0], (sem + 4 * o, sem + 4 * c), sibling))
        wait = []
        for s in (0, 1):
            for d in (1, 2, 3):
                wait.append(remote(t.at[0, 0], rt.at[s, d], (sem + 4 * s + d, sem + 4 * s + d), sibling))
        wait.append(remote(t.at[0, 0], rt.at[o, 0], (sem + 4 * o, sem + 4 * o), sibling))
        return out, wait

    thr_a = third("z", ta, rta, S_P3)
    thr_f = third("z", tf, rtf, S_P3 + 8)
    thr_b = third("y", tb, rtb, S_P3 + 16)
    thr_c = third("x", tc, rtc, S_P3 + 24)

    def begin(copies):
        for cp in copies:
            cp.start()

    def pairs(q, s):
        for p in range(2):
            for xx in range(4):
                lo = 320 * p + 40 * xx
                q[xx, 80 * p:80 * (p + 1)] = jnp.concatenate(
                    [s[lo:lo + 40], s[lo + 160:lo + 200]], axis=0).astype(BF)

    def gather(sec, q, rq, mine, s2, rows):
        for cp in sec:
            cp.wait_recv()
        r = pl.ds(0, rows)
        s2[r] = up32(q[mine, r]) + up32(rq[0, r]) + up32(rq[1, r]) + up32(rq[2, r])

    def rows36(s2, t, owners=(0, 1, 2, 3)):
        for n, owner in enumerate(owners):
            for cc in range(2):
                lo = 72 * n + 36 * cc
                t[owner, cc] = s2[lo:lo + 48].astype(BF)

    def fives(s2, t):
        for p in range(2):
            for n in range(4):
                for cc in range(2):
                    lo = 80 * p + 10 * n + 5 * cc
                    t[n, cc, 16 * p:16 * (p + 1)] = jnp.concatenate(
                        [s2[lo:lo + 8], s2[lo + 40:lo + 48]], axis=0).astype(BF)

    @pl.when(c == 1)
    def _():
        ring_relay("G")
        du(0, 1)

    for part in late:
        ring_near(part)

    @pl.when(c == 0)
    def _():
        du(0, 1)
        ring_near("F0")
        ring_near("F1")

    du(1, 3)
    for part in late:
        ring_relay(part)

    @pl.when(c == 0)
    def _():
        ring_relay("F0")
        ring_relay("F1")
    ring_end("A")
    for h in range(2):
        sa[320 * h:320 * (h + 1)] = up32(pa[y, 320 * h:320 * (h + 1)]) + up32(rfa[0, 1 - h]) + up32(rfa[1, h])
    pairs(qa, sa)
    begin(sec_a)


    s2a[160:168] = jnp.zeros((8, 128), F32)
    s2f[288:304] = jnp.zeros((16, 128), F32)
    s2b[288:304] = jnp.zeros((16, 128), F32)
    s2c[288:304] = jnp.zeros((16, 128), F32)
    def sum_pieces(p, i, rf, to, pieces):
        for first, off, rows in pieces:
            for h in range(2):
                r, f = pl.ds(first + rows * h, rows), pl.ds(off, rows)
                to[r] = up32(p[i, r]) + up32(rf[0, 1 - h, f]) + up32(rf[1, h, f])

    ring_end("B0")
    ring_end("B1")
    ring_end("B2")
    sum_pieces(pb, x, rfb, sb, PIECES)
    for h in range(2):
        for zz in range(4):
            lo = 576 * h + 72 * zz
            qb[zz, 144 * h:144 * (h + 1)] = jnp.concatenate(
                [sb[lo:lo + 72], sb[lo + 288:lo + 360]], axis=0).astype(BF)
    begin(sec_b)

    ring_end("C0")
    ring_end("C1")
    ring_end("C2")
    sum_pieces(pc, z, rfc, sc, PIECES)
    for yy in range(4):
        for xp in range(2):
            lo = row_c(yy, xp)
            qc[yy, 144 * xp:144 * (xp + 1)] = sc[lo:lo + 144].astype(BF)
    begin(sec_c)

    @pl.when(c == 0)
    def _():
        ring_end("F0")
        ring_end("F1")
        sum_pieces(pf, y, rff, sf, PIECES_F)
        for xx in range(4):
            qf[xx] = sf[288 * xx:288 * (xx + 1)].astype(BF)
        begin(sec_f)

    @pl.when(c == 1)
    def _():
        ring_end("G")
        sum_pieces(pf, y, rff, sf, ((0, 0, 320),))
        pairs(qf, sf)
        begin(sec_g)

    du(3, 6)
    store_ig = local(ig, ig_hbm.at[0], 6)
    store_ig.start()
    gather(sec_a, qa, rqa, x, s2a, 160)
    fives(s2a, ta)
    begin(thr_a[0])
    rta[c, 0] = ta[z, c]

    mid = jnp.where(x < 2, 1, 0)
    for sec, thr, q, rq, mine, s2, t, rt, i, owners in (
            (sec_b, thr_b, qb, rqb, z, s2b, tb, rtb, y, (1 + mid, 0, 2 - mid, 3)),
            (sec_c, thr_c, qc, rqc, y, s2c, tc, rtc, x, (0, 1, 2, 3))):
        gather(sec, q, rq, mine, s2, 288)
        rows36(s2, t, owners)
        begin(thr[0])
        rt[c, 0] = t[i, c]

    @pl.when(c == 0)
    def _():
        gather(sec_f, qf, rqf, x, s2f, 288)
        rows36(s2f, tf)

    @pl.when(c == 1)
    def _():
        gather(sec_g, qf, rqf, x, s2f, 160)
        s2f[160:168] = jnp.zeros((8, 128), F32)
        fives(s2f, tf)
        for n in range(4):
            for cc in range(2):
                tf[n, cc, 32:48] = jnp.zeros((16, 128), BF)

    begin(thr_f[0])
    rtf[c, 0] = tf[z, c]

    scale = 1.0 / (4 * 8192) ** 0.5

    def total(thr, rt):
        for cp in thr[1]:
            cp.wait_recv()
        return [(up32(rt[s, 0]) + up32(rt[s, 1]) + up32(rt[s, 2]) + up32(rt[s, 3])) * scale for s in range(2)]

    def put_proj(v, first):
        for b in range(4):
            po_ref[:, 128 * (first + b):128 * (first + b + 1)] = v[8 * b:8 * b + 5]

    low, high = total(thr_a, rta)
    put_proj(low, 0)
    put_proj(high, 4)
    for s, v in enumerate(total(thr_b, rtb)):
        fo_ref[:, 256 * s:256 * s + 128] = v[0:36]
    for s, v in enumerate(total(thr_c, rtc)):
        fo_ref[:, 256 * s + 128:256 * s + 256] = v[0:36]
    low, high = total(thr_f, rtf)
    fo_ref[:, 512:640] = low[0:36]
    put_proj(high, 8)

    @pl.when(has_next)
    def _():
        halo_up.wait_send()
        dz_up.wait_send()

    @pl.when(has_prev)
    def _():
        halo_dn.wait_send()
        dz_dn.wait_send()

    for cp in (sib_c, sib_u, sib_g, sib_d, sib_lo, sib_hi):
        cp.wait_send()
    def ring_left(part):
        for k in (0, 1):
            for w in range(3):
                steps[part][k][w].wait_send()

    ring_left("A")
    for part in ("B0", "C0") + late:
        ring_left(part)

    @pl.when(c == 0)
    def _():
        ring_left("F0")
        ring_left("F1")
        for cp in sec_f:
            cp.wait_send()

    @pl.when(c == 1)
    def _():
        ring_left("G")
        for cp in sec_g:
            cp.wait_send()

    for cp in sec_a + sec_b + sec_c + thr_a[0] + thr_f[0] + thr_b[0] + thr_c[0]:
        cp.wait_send()
    store_ig.wait()


def finish(*refs):
    ins, outs, held, sem = refs[:3], refs[3:6], refs[6:9], refs[9]
    come = [pltpu.make_async_copy(a, v, sem.at[i]) for i, (a, v) in enumerate(zip(ins, held))]
    go = [pltpu.make_async_copy(v, b, sem.at[3 + i]) for i, (v, b) in enumerate(zip(held, outs))]
    for cp in come:
        cp.start()
    for cp, then in zip(come, go):
        cp.wait()
        then.start()
    for cp in go:
        cp.wait()


def shards(inputs, cotangent, filter_weight, projection_weight):
    v = pltpu.VMEM
    anywhere = pl.BlockSpec(memory_space=pl.ANY)
    whole = pl.BlockSpec(memory_space=pltpu.VMEM)
    scratch = [
        v((T, C), BF), v((T, C), BF), v((2, C, T), BF), v((2 * T, C), BF), v((3 * C, H), BF), v((H, C), BF),
        v((2, D, H), BF), v((2, D, H), BF), v((T, H), F32), v((T, H), F32), v((T, H), BF),
        v((2, H, T), BF), v((2, T + 2 * D, H), BF), v((2, T + 2 * D, 384), BF),
        v((4, 640, 128), BF), v((4, 1152, 128), BF), v((4, 1152, 128), BF), v((4, 1152, 128), BF),
        v((2, 320, 128), BF), v((2, 576, 128), BF), v((2, 576, 128), BF), v((2, 576, 128), BF),
        v((2, 2, 320, 128), BF), v((2, 2, 576, 128), BF), v((2, 2, 576, 128), BF), v((2, 2, 576, 128), BF),
        v((640, 128), F32), v((1152, 128), F32), v((1152, 128), F32), v((1152, 128), F32),
        v((4, 160, 128), BF), v((4, 288, 128), BF), v((4, 288, 128), BF), v((4, 288, 128), BF),
        v((3, 160, 128), BF), v((3, 288, 128), BF), v((3, 288, 128), BF), v((3, 288, 128), BF),
        v((168, 128), F32), v((304, 128), F32), v((304, 128), F32), v((304, 128), F32),
        v((4, 2, 32, 128), BF), v((4, 2, 48, 128), BF), v((4, 2, 48, 128), BF), v((4, 2, 48, 128), BF),
        v((2, 4, 32, 128), BF), v((2, 4, 48, 128), BF), v((2, 4, 48, 128), BF), v((2, 4, 48, 128), BF),
        v((T, C), BF),
        pltpu.SemaphoreType.DMA((8,)), pltpu.SemaphoreType.DMA((N_SEM,)), pltpu.SemaphoreType.DMA((N_SEM,)),
    ]
    shapes = (
        jax.ShapeDtypeStruct((1, T, C), BF),
        jax.ShapeDtypeStruct((36, H), F32),
        jax.ShapeDtypeStruct((5, C), F32),
    )
    results = pl.pallas_call(
        kernel,
        name="block_backward",
        out_shape=shapes,
        in_specs=[anywhere] * 4,
        out_specs=(anywhere, whole, whole),
        scratch_shapes=scratch,
        compiler_params=pltpu.CompilerParams(
            collective_id=0, has_side_effects=True, vmem_limit_bytes=56 * 2**20),
        cost_estimate=pl.CostEstimate(flops=5_600_000_000, bytes_accessed=12_000_000, transcendentals=1_000_000),
    )(inputs, cotangent, filter_weight, projection_weight)
    return pl.pallas_call(
        finish,
        name="hand_out",
        out_shape=shapes,
        in_specs=[anywhere] * 3,
        out_specs=[anywhere] * 3,
        scratch_shapes=[v(s.shape, s.dtype) for s in shapes] + [pltpu.SemaphoreType.DMA((6,))],
    )(*results)


def solution(mesh):
    in_specs = (P("grp", "seq", None), P("grp", "seq", None), P(), P())
    out_specs = (P("grp", "seq", None), P(("seq", "grp"), None), P(("seq", "grp"), None))
    return jax.shard_map(shards, mesh=mesh, in_specs=in_specs, out_specs=out_specs, check_vma=False)
```

```python
import jax
import jax.numpy as jnp
from jax import lax
from jax.experimental import pallas as pl
from jax.experimental.pallas import tpu as pltpu
from jax.sharding import PartitionSpec as P

MESH = pl.DeviceIdType.MESH
BF, F32 = jnp.bfloat16, jnp.float32
D = 64
T = 256
C = 1536
H = 640
COEFF = 0.7978845608028654
NT = (((1,), (1,)), ((), ()))

S_HALO = 0
S_DZ = 2
S_SIB = 4
S_P1 = 10
S_P2 = 64
S_P3 = 76
N_SEM = 108


PIECES = ((0, 0, 144), (288, 144, 224), (736, 368, 208))
PIECES_F = ((0, 0, 144), (288, 144, 144))


def slot_b(xx, yy):
    if yy == (2 if xx < 2 else 1):
        return 0
    return {0: 1, 1: 2, 2: 2, 3: 3}[yy]


def row_c(yy, xp):
    return 144 * ((1, 1), (2, 0), (0, 0), (0, 1), (1, 0), (2, 1), (3, 0), (3, 1)).index((yy, xp))


def tanh_of(v):
    return jnp.tanh(COEFF * (v + 0.044715 * (v * v * v)))


def slope(v, t):
    return 0.5 * (1.0 + t) + 0.5 * v * (1.0 - t * t) * COEFF * (1.0 + 3.0 * 0.044715 * v * v)


def dot(a, b):
    return jnp.dot(a, b, preferred_element_type=F32)


def dot_nt(a, b):
    return lax.dot_general(a, b, NT, preferred_element_type=F32)


def up32(v):
    return v.astype(F32)


def kernel(x_hbm, cot_hbm, fw_hbm, pw_hbm, ig_hbm, fo_ref, po_ref,
           xv, ue, ut, cot, fw, pw, eo, ei, z_ref, dg_ref, g_ref, gt, dzx, dzc,
           pa, pf, pb, pc, rla, rlf, rlb, rlc, rfa, rff, rfb, rfc,
           sa, sf, sb, sc, qa, qf, qb, qc, rqa, rqf, rqb, rqc, s2a, s2f, s2b, s2c,
           ta, tf, tb, tc, rta, rtf, rtb, rtc, ig, lsem, ssem, rsem):
    seq, grp = lax.axis_index("seq"), lax.axis_index("grp")
    y, x, z, c = seq // 8, (seq // 2) % 4, (seq % 2) * 2 + grp // 2, grp % 2
    o = 1 - c

    def dev(xx, yy, zz, cc):
        return (yy * 8 + xx * 2 + zz // 2, (zz % 2) * 2 + cc)

    def at(axis, d, cc):
        xx = (x + d) % 4 if axis == "x" else x
        yy = (y + d) % 4 if axis == "y" else y
        zz = (z + d) % 4 if axis == "z" else z
        return dev(xx, yy, zz, cc)

    sibling = (seq, grp + 1 - 2 * c)
    pos = {"x": x, "y": y, "z": z}
    has_prev, has_next = seq > 0, seq < 31
    nxt, prv = (seq + 1, grp), (seq - 1, grp)

    def remote(src, dst, sem, device):
        return pltpu.make_async_remote_copy(
            src_ref=src, dst_ref=dst, send_sem=ssem.at[sem[0]], recv_sem=rsem.at[sem[1]],
            device_id=device, device_id_type=MESH)

    def local(src, dst, i):
        return pltpu.make_async_copy(src, dst, lsem.at[i])

    load_x = local(x_hbm.at[0], xv, 0)
    load_f = [local(fw_hbm.at[pl.ds(C * k, C)], fw.at[pl.ds(C * k, C)], 1 + k) for k in range(3)]
    load_c = local(cot_hbm.at[0], cot.at[pl.ds(0, T)], 4)
    load_p = local(pw_hbm, pw, 5)
    load_x.start()
    load_f[0].start()
    load_f[2].start()

    barrier = pltpu.get_barrier_semaphore()

    def greet(device):
        pl.semaphore_signal(barrier, inc=1, device_id=device, device_id_type=MESH)

    @pl.when(has_next)
    def _():
        greet(nxt)

    @pl.when(has_prev)
    def _():
        greet(prv)

    greet(sibling)
    for axis in ("x", "y", "z"):
        for d in (1, 2, 3):
            for cc in (0, 1):
                greet(at(axis, d, cc))

    def act(first, rows):
        v = up32(xv[pl.ds(first, rows)])
        ue[pl.ds(first, rows)] = (0.5 * v * (1.0 + tanh_of(v))).astype(BF)

    load_x.wait()
    for first in (192, 224, 0, 32):
        act(first, 32)
    pl.semaphore_wait(barrier, 19 + has_prev.astype(jnp.int32) + has_next.astype(jnp.int32))
    halo_up = remote(eo.at[0], ei.at[0], (S_HALO, S_HALO), nxt)
    halo_dn = remote(eo.at[1], ei.at[1], (S_HALO + 1, S_HALO + 1), prv)
    dz_up = remote(dzx.at[0, pl.ds(T, D)], dzx.at[0, pl.ds(0, D)], (S_DZ, S_DZ), nxt)
    dz_dn = remote(dzx.at[0, pl.ds(D, D)], dzx.at[0, pl.ds(D + T, D)], (S_DZ + 1, S_DZ + 1), prv)

    load_f[0].wait()
    eo[0] = dot(ue[T - D:T], fw[0:C]).astype(BF)

    @pl.when(has_next)
    def _():
        halo_up.start()

    load_f[2].wait()
    load_f[1].start()
    load_c.start()
    load_p.start()
    eo[1] = dot(ue[0:D], fw[2 * C:3 * C]).astype(BF)

    @pl.when(has_prev)
    def _():
        halo_dn.start()

    sib_c = remote(cot_hbm.at[0], cot.at[pl.ds(T, T)], (S_SIB, S_SIB), sibling)
    sib_u = remote(ut.at[0], ut.at[1], (S_SIB + 1, S_SIB + 1), sibling)
    sib_g = remote(gt.at[0], gt.at[1], (S_SIB + 2, S_SIB + 2), sibling)

    def sib_dz(first, rows, sem):
        return remote(dzx.at[0, pl.ds(first, rows)], dzx.at[1, pl.ds(first, rows)], (sem, sem), sibling)

    sib_d = sib_dz(D, T, S_SIB + 3)
    sib_lo = sib_dz(0, D, S_SIB + 4)
    sib_hi = sib_dz(D + T, D, S_SIB + 5)
    sib_c.start()

    @pl.loop(0, 4)
    def _(i):
        act(pl.multiple_of(D + i * 32, 32), 32)

    ut[0, :, 0:128] = ue[0:128].T
    ut[0, :, 128:256] = ue[128:256].T
    sib_u.start()

    load_f[1].wait()
    z_ref[...] = dot(ue[...], fw[C:2 * C])
    z_ref[64:256] += dot(ue[0:192], fw[0:C])
    z_ref[0:192] += dot(ue[64:256], fw[2 * C:3 * C])
    load_c.wait()
    load_p.wait()
    dg_ref[...] = dot_nt(cot[0:T], pw[...])

    def inner(first):
        rows = pl.ds(first, 32)
        v = z_ref[rows]
        t = tanh_of(v)
        g_ref[rows] = (0.5 * v * (1.0 + t)).astype(BF)
        dzx[0, pl.ds(D + first, 32)] = (dg_ref[rows] * slope(v, t)).astype(BF)

    for first in (64, 96, 128, 160):
        inner(first)

    @pl.when(has_prev)
    def _():
        halo_up.wait_recv()
        z_ref[0:64] += up32(ei[0])

    inner(0)
    inner(32)

    @pl.when(has_prev)
    def _():
        dz_dn.start()

    @pl.when(has_next)
    def _():
        halo_dn.wait_recv()
        z_ref[192:256] += up32(ei[1])

    inner(192)
    inner(224)

    @pl.when(has_next)
    def _():
        dz_up.start()

    gt[0] = g_ref[...].T
    sib_g.start()
    sib_d.start()

    def flat(p, first, rows):
        return lambda j, h: p.at[j, pl.ds(first + rows * h, rows)]

    def cut(r, first, rows):
        return r.at[..., pl.ds(first, rows), :]

    rings = {
        "A": ("y", flat(pa, 0, 480), rla, rfa, S_P1),
    }
    for n, (first, off, rows) in enumerate(PIECES_F):
        rings[f"F{n}"] = ("y", flat(pf, first, rows), cut(rlf, off, rows), cut(rff, off, rows), S_P1 + 6 + 6 * n)
    for n, (first, off, rows) in enumerate(PIECES):
        rings[f"B{n}"] = ("x", flat(pb, first, rows), cut(rlb, off, rows), cut(rfb, off, rows), S_P1 + 18 + 6 * n)
        rings[f"C{n}"] = ("z", flat(pc, first, rows), cut(rlc, off, rows), cut(rfc, off, rows), S_P1 + 36 + 6 * n)

    def ring(part):
        axis, chunk, rl, rf, sem = rings[part]
        i = pos[axis]
        up, far, dn = (i + 1) % 4, (i + 2) % 4, (i + 3) % 4
        out = []
        for k, (near, h, to) in enumerate(((up, 0, 1), (dn, 1, 3))):
            who = at(axis, to, c)
            s = sem + 3 * k
            out.append((
                remote(chunk(far, h), rl.at[k], (s, s), who),
                remote(chunk(near, 1 - h), rf.at[k, 0], (s + 1, s + 1), who),
                remote(chunk(near, h), rf.at[k, 1], (s + 2, s + 2), who),
                chunk(near, h), rl.at[k]))
        return out

    steps = {part: ring(part) for part in rings}

    def ring_far(part):
        for k in (0, 1):
            steps[part][k][0].start()

    def ring_near(part):
        for k in (0, 1):
            steps[part][k][1].start()

    def ring_start(part):
        ring_far(part)
        ring_near(part)

    def ring_relay(part):
        for k in (0, 1):
            first, _, second, mine, came = steps[part][k]
            first.wait_recv()
            mine[...] = (up32(mine[...]) + up32(came[...])).astype(BF)
            second.start()

    def ring_end(part):
        for k in (0, 1):
            steps[part][k][1].wait_recv()
            steps[part][k][2].wait_recv()

    def proj(to, first, n):
        cols = pl.ds(pl.multiple_of(first, 256), 256)
        acc = dot(gt[0], cot[0:T, cols]) + dot(gt[1], cot[T:2 * T, cols])
        for j in range(4):
            for b in range(2):
                to[j, 320 * n + 160 * b:320 * n + 160 * (b + 1)] = (
                    acc[160 * j:160 * (j + 1), 128 * b:128 * (b + 1)].astype(BF))

    sib_c.wait_recv()
    sib_g.wait_recv()
    for n in range(3):
        proj(pa, 768 * c + 256 * n, n)
    ring_far("A")

    def columns(s, first, rows):
        r = pl.ds(first, rows)
        dzc[s, r, 0:256] = dzx[s, r, pl.ds(pl.multiple_of(256 * c, 256), 256)]
        dzc[s, r, 256:384] = dzx[s, r, 512:640]

    def rhs(tap, lo, hi):
        r = pl.ds(D * (2 - tap), T)
        return jnp.concatenate([dzc[0, r, lo:hi], dzc[1, r, lo:hi]], axis=0)

    def rows_of(first, rows, lo, hi):
        out = []
        last = first + rows
        while first < last:
            tap = first // C
            stop = min(last, C * (tap + 1))
            r = slice(first - C * tap, stop - C * tap)
            left = jnp.concatenate([ut[0, r], ut[1, r]], axis=1)
            out.append(dot(left, rhs(tap, lo, hi)))
            first = stop
        return out[0] if len(out) == 1 else jnp.concatenate(out, axis=0)

    def filt(n):
        yy, xp = n // 2, n % 2
        acc = rows_of(576 * n, 576, 0, 256)
        for b in range(2):
            first = 288 * slot_b(2 * xp + b, yy)
            pb[2 * xp + b, first:first + 288] = acc[288 * b:288 * (b + 1), 0:128].astype(BF)
        first = row_c(yy, xp)
        for zz in range(4):
            pc[zz, first:first + 144] = jnp.concatenate(
                [acc[72 * zz:72 * zz + 72, 128:256], acc[288 + 72 * zz:360 + 72 * zz, 128:256]],
                axis=0).astype(BF)

    def filt_last(groups):
        for core in range(2):
            @pl.when(c == core)
            def _():
                for n in groups:
                    pf[n // 4, 144 * (n % 4):144 * (n % 4 + 1)] = (
                        rows_of(288 * n + 144 * core, 144, 256, 384).astype(BF))

    columns(0, D, T)
    sib_u.wait_recv()
    sib_d.wait_recv()
    columns(1, D, T)
    filt(3)
    filt(4)
    ring_start("B0")
    ring_near("A")
    filt_last((6, 7, 8, 9))
    @pl.when(has_prev)
    def _():
        dz_up.wait_recv()

    @pl.when(jnp.logical_not(has_prev))
    def _():
        dzx[0, 0:D] = jnp.zeros((D, H), BF)

    sib_lo.start()

    @pl.when(has_next)
    def _():
        dz_dn.wait_recv()

    @pl.when(jnp.logical_not(has_next))
    def _():
        dzx[0, D + T:D + T + D] = jnp.zeros((D, H), BF)

    sib_hi.start()
    columns(0, 0, D)
    columns(0, D + T, D)
    ring_start("C0")
    ring_relay("B0")
    sib_lo.wait_recv()
    sib_hi.wait_recv()
    columns(1, 0, D)
    columns(1, D + T, D)
    late = ("B1", "C1", "B2", "C2")
    for n in (0, 1, 2, 5):
        filt(n)
    ring_far("B1")
    ring_far("C1")
    ring_relay("A")
    for n in (6, 7):
        filt(n)
    ring_far("B2")
    ring_far("C2")
    ring_relay("C0")
    filt_last((0, 1, 2, 3, 4, 5, 10, 11, 12, 13, 14, 15))
    ring_far("F0")
    ring_far("F1")

    def du(lo, hi):
        @pl.loop(lo, hi)
        def _(n):
            cols = pl.ds(pl.multiple_of(256 * n, 256), 256)
            acc = jnp.zeros((T, 256), F32)
            for k in range(3):
                rows = pl.ds(pl.multiple_of(C * k + 256 * n, 256), 256)
                acc += dot_nt(dzx[0, D * (2 - k):D * (2 - k) + T], fw[rows])
            v = up32(xv[:, cols])
            ig[:, cols] = (up32(cot[0:T, cols]) + acc * slope(v, tanh_of(v))).astype(BF)

    def second(axis, q, rq, sem):
        return [remote(q.at[(pos[axis] + d) % 4], rq.at[d - 1], (sem + d - 1, sem + d - 1), at(axis, d, c))
                for d in (1, 2, 3)]

    sec_a = second("x", qa, rqa, S_P2)
    sec_f = second("x", qf, rqf, S_P2 + 3)
    sec_b = second("z", qb, rqb, S_P2 + 6)
    sec_c = second("y", qc, rqc, S_P2 + 9)

    def third(axis, t, rt, sem):
        i = pos[axis]
        out = []
        for d in (2, 1, 3):
            for cc in (0, 1):
                out.append(remote(t.at[(i + d) % 4, cc], rt.at[c, d],
                                  (sem + 4 * cc + d, sem + 4 * c + d), at(axis, d, cc)))
        out.append(remote(t.at[i, o], rt.at[c, 0], (sem + 4 * o, sem + 4 * c), sibling))
        wait = []
        for s in (0, 1):
            for d in (1, 2, 3):
                wait.append(remote(t.at[0, 0], rt.at[s, d], (sem + 4 * s + d, sem + 4 * s + d), sibling))
        wait.append(remote(t.at[0, 0], rt.at[o, 0], (sem + 4 * o, sem + 4 * o), sibling))
        return out, wait

    thr_a = third("z", ta, rta, S_P3)
    s_f = S_P3 + 8
    half = z // 2
    to_f = [[remote(tf.at[(z + d) % 4, cc], rtf.at[c, d], (s_f + 4 * cc + d, s_f + 4 * c + d), at("z", d, cc))
             for cc in (0, 1)] for d in (1, 2, 3)]
    to_sib = remote(tf.at[z, o], rtf.at[c, 0], (s_f + 4 * o, s_f + 4 * c), sibling)
    from_f = [remote(tf.at[0, 0], rtf.at[half, d], (s_f + 4 * half + d, s_f + 4 * half + d), sibling)
              for d in (1, 2, 3)]
    from_sib = remote(tf.at[0, 0], rtf.at[o, 0], (s_f + 4 * o, s_f + 4 * o), sibling)

    def each_to_f(do):
        for d in (1, 2, 3):
            @pl.when(((z + d) % 4) // 2 == c)
            def _():
                for cp in to_f[d - 1]:
                    do(cp)

    thr_b = third("y", tb, rtb, S_P3 + 16)
    thr_c = third("x", tc, rtc, S_P3 + 24)

    def begin(copies):
        for cp in copies:
            cp.start()

    def pairs(q, s):
        for p in range(3):
            for xx in range(4):
                lo = 320 * p + 40 * xx
                q[xx, 80 * p:80 * (p + 1)] = jnp.concatenate(
                    [s[lo:lo + 40], s[lo + 160:lo + 200]], axis=0).astype(BF)

    def gather(sec, q, rq, mine, s2, rows):
        for cp in sec:
            cp.wait_recv()
        r = pl.ds(0, rows)
        s2[r] = up32(q[mine, r]) + up32(rq[0, r]) + up32(rq[1, r]) + up32(rq[2, r])

    def rows36(s2, t, owners=(0, 1, 2, 3)):
        for n, owner in enumerate(owners):
            for cc in range(2):
                lo = 72 * n + 36 * cc
                t[owner, cc] = s2[lo:lo + 48].astype(BF)

    def fives(s2, t):
        for p in range(3):
            for n in range(4):
                for cc in range(2):
                    lo = 80 * p + 10 * n + 5 * cc
                    t[n, cc, 16 * p:16 * (p + 1)] = jnp.concatenate(
                        [s2[lo:lo + 8], s2[lo + 40:lo + 48]], axis=0).astype(BF)

    du(0, 1)
    for part in late:
        ring_near(part)
    ring_near("F0")
    ring_near("F1")
    du(1, 3)
    for part in late:
        ring_relay(part)
    ring_relay("F0")
    ring_relay("F1")


    s2a[240:248] = jnp.zeros((8, 128), F32)
    s2f[144:160] = jnp.zeros((16, 128), F32)
    s2b[288:304] = jnp.zeros((16, 128), F32)
    s2c[288:304] = jnp.zeros((16, 128), F32)
    def sum_pieces(p, i, rf, to, pieces):
        for first, off, rows in pieces:
            for h in range(2):
                r, f = pl.ds(first + rows * h, rows), pl.ds(off, rows)
                to[r] = up32(p[i, r]) + up32(rf[0, 1 - h, f]) + up32(rf[1, h, f])

    ring_end("A")
    sum_pieces(pa, y, rfa, sa, ((0, 0, 480),))
    pairs(qa, sa)
    begin(sec_a)

    ring_end("B0")
    ring_end("B1")
    ring_end("B2")
    sum_pieces(pb, x, rfb, sb, PIECES)
    for h in range(2):
        for zz in range(4):
            lo = 576 * h + 72 * zz
            qb[zz, 144 * h:144 * (h + 1)] = jnp.concatenate(
                [sb[lo:lo + 72], sb[lo + 288:lo + 360]], axis=0).astype(BF)
    begin(sec_b)

    ring_end("C0")
    ring_end("C1")
    ring_end("C2")
    sum_pieces(pc, z, rfc, sc, PIECES)
    for yy in range(4):
        for xp in range(2):
            lo = row_c(yy, xp)
            qc[yy, 144 * xp:144 * (xp + 1)] = sc[lo:lo + 144].astype(BF)
    begin(sec_c)

    ring_end("F0")
    ring_end("F1")
    sum_pieces(pf, y, rff, sf, PIECES_F)
    for xx in range(4):
        qf[xx] = sf[144 * xx:144 * (xx + 1)].astype(BF)
    begin(sec_f)
    du(3, 6)
    store_ig = local(ig, ig_hbm.at[0], 6)
    store_ig.start()
    gather(sec_a, qa, rqa, x, s2a, 240)
    fives(s2a, ta)
    begin(thr_a[0])
    rta[c, 0] = ta[z, c]

    mid = jnp.where(x < 2, 1, 0)
    for sec, thr, q, rq, mine, s2, t, rt, i, owners in (
            (sec_b, thr_b, qb, rqb, z, s2b, tb, rtb, y, (1 + mid, 0, 2 - mid, 3)),
            (sec_c, thr_c, qc, rqc, y, s2c, tc, rtc, x, (0, 1, 2, 3))):
        gather(sec, q, rq, mine, s2, 288)
        rows36(s2, t, owners)
        begin(thr[0])
        rt[c, 0] = t[i, c]

    gather(sec_f, qf, rqf, x, s2f, 144)
    for n in range(2):
        for cc in range(2):
            lo = 72 * n + 36 * cc
            tf[2 * c + n, cc] = s2f[lo:lo + 48].astype(BF)
    each_to_f(lambda cp: cp.start())

    @pl.when(half == c)
    def _():
        to_sib.start()
        rtf[c, 0] = tf[z, c]

    scale = 1.0 / (4 * 8192) ** 0.5

    def total(thr, rt):
        for cp in thr[1]:
            cp.wait_recv()
        return [(up32(rt[s, 0]) + up32(rt[s, 1]) + up32(rt[s, 2]) + up32(rt[s, 3])) * scale for s in range(2)]

    for s, v in enumerate(total(thr_a, rta)):
        for b in range(6):
            po_ref[:, 768 * s + 128 * b:768 * s + 128 * (b + 1)] = v[8 * b:8 * b + 5]
    for s, v in enumerate(total(thr_b, rtb)):
        fo_ref[:, 256 * s:256 * s + 128] = v[0:36]
    for s, v in enumerate(total(thr_c, rtc)):
        fo_ref[:, 256 * s + 128:256 * s + 256] = v[0:36]
    for cp in from_f:
        cp.wait_recv()

    @pl.when(half != c)
    def _():
        from_sib.wait_recv()

    last = up32(rtf[half, 0]) + up32(rtf[half, 1]) + up32(rtf[half, 2]) + up32(rtf[half, 3])
    fo_ref[:, 512:640] = (last * scale)[0:36]

    @pl.when(has_next)
    def _():
        halo_up.wait_send()
        dz_up.wait_send()

    @pl.when(has_prev)
    def _():
        halo_dn.wait_send()
        dz_dn.wait_send()

    for cp in (sib_c, sib_u, sib_g, sib_d, sib_lo, sib_hi):
        cp.wait_send()
    def ring_left(part):
        for k in (0, 1):
            for w in range(3):
                steps[part][k][w].wait_send()

    ring_left("A")
    for part in ("B0", "C0", "F0", "F1") + late:
        ring_left(part)

    each_to_f(lambda cp: cp.wait_send())

    @pl.when(half == c)
    def _():
        to_sib.wait_send()

    for cp in sec_a + sec_f + sec_b + sec_c + thr_a[0] + thr_b[0] + thr_c[0]:
        cp.wait_send()
    store_ig.wait()


def finish(*refs):
    ins, outs, held, sem = refs[:3], refs[3:6], refs[6:9], refs[9]
    come = [pltpu.make_async_copy(a, v, sem.at[i]) for i, (a, v) in enumerate(zip(ins, held))]
    go = [pltpu.make_async_copy(v, b, sem.at[3 + i]) for i, (v, b) in enumerate(zip(held, outs))]
    for cp in come:
        cp.start()
    for cp, then in zip(come, go):
        cp.wait()
        then.start()
    for cp in go:
        cp.wait()


def shards(inputs, cotangent, filter_weight, projection_weight):
    v = pltpu.VMEM
    anywhere = pl.BlockSpec(memory_space=pl.ANY)
    whole = pl.BlockSpec(memory_space=pltpu.VMEM)
    scratch = [
        v((T, C), BF), v((T, C), BF), v((2, C, T), BF), v((2 * T, C), BF), v((3 * C, H), BF), v((H, C), BF),
        v((2, D, H), BF), v((2, D, H), BF), v((T, H), F32), v((T, H), F32), v((T, H), BF),
        v((2, H, T), BF), v((2, T + 2 * D, H), BF), v((2, T + 2 * D, 384), BF),
        v((4, 960, 128), BF), v((4, 576, 128), BF), v((4, 1152, 128), BF), v((4, 1152, 128), BF),
        v((2, 480, 128), BF), v((2, 288, 128), BF), v((2, 576, 128), BF), v((2, 576, 128), BF),
        v((2, 2, 480, 128), BF), v((2, 2, 288, 128), BF), v((2, 2, 576, 128), BF), v((2, 2, 576, 128), BF),
        v((960, 128), F32), v((576, 128), F32), v((1152, 128), F32), v((1152, 128), F32),
        v((4, 240, 128), BF), v((4, 144, 128), BF), v((4, 288, 128), BF), v((4, 288, 128), BF),
        v((3, 240, 128), BF), v((3, 144, 128), BF), v((3, 288, 128), BF), v((3, 288, 128), BF),
        v((248, 128), F32), v((160, 128), F32), v((304, 128), F32), v((304, 128), F32),
        v((4, 2, 48, 128), BF), v((4, 2, 48, 128), BF), v((4, 2, 48, 128), BF), v((4, 2, 48, 128), BF),
        v((2, 4, 48, 128), BF), v((2, 4, 48, 128), BF), v((2, 4, 48, 128), BF), v((2, 4, 48, 128), BF),
        v((T, C), BF),
        pltpu.SemaphoreType.DMA((8,)), pltpu.SemaphoreType.DMA((N_SEM,)), pltpu.SemaphoreType.DMA((N_SEM,)),
    ]
    shapes = (
        jax.ShapeDtypeStruct((1, T, C), BF),
        jax.ShapeDtypeStruct((36, H), F32),
        jax.ShapeDtypeStruct((5, C), F32),
    )
    results = pl.pallas_call(
        kernel,
        name="block_backward",
        out_shape=shapes,
        in_specs=[anywhere] * 4,
        out_specs=(anywhere, whole, whole),
        scratch_shapes=scratch,
        compiler_params=pltpu.CompilerParams(
            collective_id=0, has_side_effects=True, vmem_limit_bytes=56 * 2**20),
        cost_estimate=pl.CostEstimate(flops=5_600_000_000, bytes_accessed=12_000_000, transcendentals=1_000_000),
    )(inputs, cotangent, filter_weight, projection_weight)
    return pl.pallas_call(
        finish,
        name="hand_out",
        out_shape=shapes,
        in_specs=[anywhere] * 3,
        out_specs=[anywhere] * 3,
        scratch_shapes=[v(s.shape, s.dtype) for s in shapes] + [pltpu.SemaphoreType.DMA((6,))],
    )(*results)


def solution(mesh):
    in_specs = (P("grp", "seq", None), P("grp", "seq", None), P(), P())
    out_specs = (P("grp", "seq", None), P(("seq", "grp"), None), P(("seq", "grp"), None))
    return jax.shard_map(shards, mesh=mesh, in_specs=in_specs, out_specs=out_specs, check_vma=False)
```

```python
import jax
import jax.numpy as jnp
from jax import lax
from jax.experimental import pallas as pl
from jax.experimental.pallas import tpu as pltpu
from jax.sharding import PartitionSpec as P

MESH = pl.DeviceIdType.MESH
BF, F32 = jnp.bfloat16, jnp.float32
D = 64
T = 256
C = 1536
H = 640
COEFF = 0.7978845608028654
NT = (((1,), (1,)), ((), ()))

S_HALO = 0
S_DZ = 2
S_SIB = 4
S_P1 = 10
S_P2 = 64
S_P3 = 76
N_SEM = 108


PIECES = ((0, 0, 144), (288, 144, 224), (736, 368, 208))
PIECES_F = ((0, 0, 144), (288, 144, 144))


def slot_b(xx, yy):
    if yy == (2 if xx < 2 else 1):
        return 0
    return {0: 1, 1: 2, 2: 2, 3: 3}[yy]


def row_c(yy, xp):
    return 144 * ((1, 1), (2, 0), (0, 0), (0, 1), (1, 0), (2, 1), (3, 0), (3, 1)).index((yy, xp))


def tanh_of(v):
    return jnp.tanh(COEFF * (v + 0.044715 * (v * v * v)))


def slope(v, t):
    return 0.5 * (1.0 + t) + 0.5 * v * (1.0 - t * t) * COEFF * (1.0 + 3.0 * 0.044715 * v * v)


def dot(a, b):
    return jnp.dot(a, b, preferred_element_type=F32)


def dot_nt(a, b):
    return lax.dot_general(a, b, NT, preferred_element_type=F32)


def up32(v):
    return v.astype(F32)


def kernel(x_hbm, cot_hbm, fw_hbm, pw_hbm, ig_hbm, fo_ref, po_ref,
           xv, ue, ut, cot, fw, pw, eo, ei, z_ref, dg_ref, g_ref, gt, dzx, dzc,
           pa, pf, pb, pc, rla, rlf, rlb, rlc, rfa, rff, rfb, rfc,
           sa, sf, sb, sc, qa, qf, qb, qc, rqa, rqf, rqb, rqc, s2a, s2f, s2b, s2c,
           ta, tf, tb, tc, rta, rtf, rtb, rtc, ig, lsem, ssem, rsem):
    seq, grp = lax.axis_index("seq"), lax.axis_index("grp")
    y, x, z, c = seq // 8, (seq // 2) % 4, (seq % 2) * 2 + grp // 2, grp % 2
    o = 1 - c

    def dev(xx, yy, zz, cc):
        return (yy * 8 + xx * 2 + zz // 2, (zz % 2) * 2 + cc)

    def at(axis, d, cc):
        xx = (x + d) % 4 if axis == "x" else x
        yy = (y + d) % 4 if axis == "y" else y
        zz = (z + d) % 4 if axis == "z" else z
        return dev(xx, yy, zz, cc)

    sibling = (seq, grp + 1 - 2 * c)
    pos = {"x": x, "y": y, "z": z}
    has_prev, has_next = seq > 0, seq < 31
    nxt, prv = (seq + 1, grp), (seq - 1, grp)

    def remote(src, dst, sem, device):
        return pltpu.make_async_remote_copy(
            src_ref=src, dst_ref=dst, send_sem=ssem.at[sem[0]], recv_sem=rsem.at[sem[1]],
            device_id=device, device_id_type=MESH)

    def local(src, dst, i):
        return pltpu.make_async_copy(src, dst, lsem.at[i])

    load_x = local(x_hbm.at[0], xv, 0)
    load_f = [local(fw_hbm.at[pl.ds(C * k, C)], fw.at[pl.ds(C * k, C)], 1 + k) for k in range(3)]
    load_c = local(cot_hbm.at[0], cot.at[pl.ds(0, T)], 4)
    load_p = local(pw_hbm, pw, 5)
    load_x.start()
    load_f[0].start()
    load_f[2].start()

    barrier = pltpu.get_barrier_semaphore()

    def greet(device):
        pl.semaphore_signal(barrier, inc=1, device_id=device, device_id_type=MESH)

    @pl.when(has_next)
    def _():
        greet(nxt)

    @pl.when(has_prev)
    def _():
        greet(prv)

    greet(sibling)
    for axis in ("x", "y", "z"):
        for d in (1, 2, 3):
            for cc in (0, 1):
                greet(at(axis, d, cc))

    def act(first, rows):
        v = up32(xv[pl.ds(first, rows)])
        ue[pl.ds(first, rows)] = (0.5 * v * (1.0 + tanh_of(v))).astype(BF)

    load_x.wait()
    for first in (192, 224, 0, 32):
        act(first, 32)
    pl.semaphore_wait(barrier, 19 + has_prev.astype(jnp.int32) + has_next.astype(jnp.int32))
    halo_up = remote(eo.at[0], ei.at[0], (S_HALO, S_HALO), nxt)
    halo_dn = remote(eo.at[1], ei.at[1], (S_HALO + 1, S_HALO + 1), prv)
    dz_up = remote(dzx.at[0, pl.ds(T, D)], dzx.at[0, pl.ds(0, D)], (S_DZ, S_DZ), nxt)
    dz_dn = remote(dzx.at[0, pl.ds(D, D)], dzx.at[0, pl.ds(D + T, D)], (S_DZ + 1, S_DZ + 1), prv)

    load_f[0].wait()
    eo[0] = dot(ue[T - D:T], fw[0:C]).astype(BF)

    @pl.when(has_next)
    def _():
        halo_up.start()

    load_f[2].wait()
    load_f[1].start()
    load_c.start()
    load_p.start()
    eo[1] = dot(ue[0:D], fw[2 * C:3 * C]).astype(BF)

    @pl.when(has_prev)
    def _():
        halo_dn.start()

    sib_c = remote(cot_hbm.at[0], cot.at[pl.ds(T, T)], (S_SIB, S_SIB), sibling)
    sib_u = remote(ut.at[0], ut.at[1], (S_SIB + 1, S_SIB + 1), sibling)
    sib_g = remote(gt.at[0], gt.at[1], (S_SIB + 2, S_SIB + 2), sibling)

    def sib_dz(first, rows, sem):
        return remote(dzx.at[0, pl.ds(first, rows)], dzx.at[1, pl.ds(first, rows)], (sem, sem), sibling)

    sib_d = sib_dz(D, T, S_SIB + 3)
    sib_lo = sib_dz(0, D, S_SIB + 4)
    sib_hi = sib_dz(D + T, D, S_SIB + 5)
    sib_c.start()

    @pl.loop(0, 4)
    def _(i):
        act(pl.multiple_of(D + i * 32, 32), 32)

    ut[0, :, 0:128] = ue[0:128].T
    ut[0, :, 128:256] = ue[128:256].T
    sib_u.start()

    load_f[1].wait()
    z_ref[...] = dot(ue[...], fw[C:2 * C])
    z_ref[64:256] += dot(ue[0:192], fw[0:C])
    z_ref[0:192] += dot(ue[64:256], fw[2 * C:3 * C])
    load_c.wait()
    load_p.wait()
    dg_ref[...] = dot_nt(cot[0:T], pw[...])

    def inner(first):
        rows = pl.ds(first, 32)
        v = z_ref[rows]
        t = tanh_of(v)
        g_ref[rows] = (0.5 * v * (1.0 + t)).astype(BF)
        dzx[0, pl.ds(D + first, 32)] = (dg_ref[rows] * slope(v, t)).astype(BF)

    for first in (64, 96, 128, 160):
        inner(first)

    @pl.when(has_prev)
    def _():
        halo_up.wait_recv()
        z_ref[0:64] += up32(ei[0])

    inner(0)
    inner(32)

    @pl.when(has_prev)
    def _():
        dz_dn.start()

    @pl.when(has_next)
    def _():
        halo_dn.wait_recv()
        z_ref[192:256] += up32(ei[1])

    inner(192)
    inner(224)

    @pl.when(has_next)
    def _():
        dz_up.start()

    gt[0] = g_ref[...].T
    sib_g.start()
    sib_d.start()

    def flat(p, first, rows):
        return lambda j, h: p.at[j, pl.ds(first + rows * h, rows)]

    def cut(r, first, rows):
        return r.at[..., pl.ds(first, rows), :]

    rings = {
        "A": ("y", flat(pa, 0, 480), rla, rfa, S_P1),
    }
    for n, (first, off, rows) in enumerate(PIECES_F):
        rings[f"F{n}"] = ("y", flat(pf, first, rows), cut(rlf, off, rows), cut(rff, off, rows), S_P1 + 6 + 6 * n)
    for n, (first, off, rows) in enumerate(PIECES):
        rings[f"B{n}"] = ("x", flat(pb, first, rows), cut(rlb, off, rows), cut(rfb, off, rows), S_P1 + 18 + 6 * n)
        rings[f"C{n}"] = ("z", flat(pc, first, rows), cut(rlc, off, rows), cut(rfc, off, rows), S_P1 + 36 + 6 * n)

    def ring(part):
        axis, chunk, rl, rf, sem = rings[part]
        i = pos[axis]
        up, far, dn = (i + 1) % 4, (i + 2) % 4, (i + 3) % 4
        out = []
        for k, (near, h, to) in enumerate(((up, 0, 1), (dn, 1, 3))):
            who = at(axis, to, c)
            s = sem + 3 * k
            out.append((
                remote(chunk(far, h), rl.at[k], (s, s), who),
                remote(chunk(near, 1 - h), rf.at[k, 0], (s + 1, s + 1), who),
                remote(chunk(near, h), rf.at[k, 1], (s + 2, s + 2), who),
                chunk(near, h), rl.at[k]))
        return out

    steps = {part: ring(part) for part in rings}

    def ring_far(part):
        for k in (0, 1):
            steps[part][k][0].start()

    def ring_near(part):
        for k in (0, 1):
            steps[part][k][1].start()

    def ring_start(part):
        ring_far(part)
        ring_near(part)

    def ring_relay(part):
        for k in (0, 1):
            first, _, second, mine, came = steps[part][k]
            first.wait_recv()
            mine[...] = (up32(mine[...]) + up32(came[...])).astype(BF)
            second.start()

    def ring_end(part):
        for k in (0, 1):
            steps[part][k][1].wait_recv()
            steps[part][k][2].wait_recv()

    def proj(to, first, n):
        cols = pl.ds(pl.multiple_of(first, 256), 256)
        acc = dot(gt[0], cot[0:T, cols]) + dot(gt[1], cot[T:2 * T, cols])
        for j in range(4):
            for b in range(2):
                to[j, 320 * n + 160 * b:320 * n + 160 * (b + 1)] = (
                    acc[160 * j:160 * (j + 1), 128 * b:128 * (b + 1)].astype(BF))

    sib_c.wait_recv()
    sib_g.wait_recv()
    for n in range(3):
        proj(pa, 768 * c + 256 * n, n)
    ring_far("A")

    def columns(s, first, rows):
        r = pl.ds(first, rows)
        dzc[s, r, 0:256] = dzx[s, r, pl.ds(pl.multiple_of(256 * c, 256), 256)]
        dzc[s, r, 256:384] = dzx[s, r, 512:640]

    def rhs(tap, lo, hi):
        r = pl.ds(D * (2 - tap), T)
        return jnp.concatenate([dzc[0, r, lo:hi], dzc[1, r, lo:hi]], axis=0)

    def rows_of(first, rows, lo, hi):
        out = []
        last = first + rows
        while first < last:
            tap = first // C
            stop = min(last, C * (tap + 1))
            r = slice(first - C * tap, stop - C * tap)
            left = jnp.concatenate([ut[0, r], ut[1, r]], axis=1)
            out.append(dot(left, rhs(tap, lo, hi)))
            first = stop
        return out[0] if len(out) == 1 else jnp.concatenate(out, axis=0)

    def filt(n):
        yy, xp = n // 2, n % 2
        acc = rows_of(576 * n, 576, 0, 256)
        for b in range(2):
            first = 288 * slot_b(2 * xp + b, yy)
            pb[2 * xp + b, first:first + 288] = acc[288 * b:288 * (b + 1), 0:128].astype(BF)
        first = row_c(yy, xp)
        for zz in range(4):
            pc[zz, first:first + 144] = jnp.concatenate(
                [acc[72 * zz:72 * zz + 72, 128:256], acc[288 + 72 * zz:360 + 72 * zz, 128:256]],
                axis=0).astype(BF)

    def filt_last(groups):
        for core in range(2):
            @pl.when(c == core)
            def _():
                for n in groups:
                    pf[n // 4, 144 * (n % 4):144 * (n % 4 + 1)] = (
                        rows_of(288 * n + 144 * core, 144, 256, 384).astype(BF))

    columns(0, D, T)
    sib_u.wait_recv()
    sib_d.wait_recv()
    columns(1, D, T)
    filt(3)
    filt(4)
    ring_start("B0")
    ring_near("A")
    filt_last((6, 7, 8, 9))
    @pl.when(has_prev)
    def _():
        dz_up.wait_recv()

    @pl.when(jnp.logical_not(has_prev))
    def _():
        dzx[0, 0:D] = jnp.zeros((D, H), BF)

    sib_lo.start()

    @pl.when(has_next)
    def _():
        dz_dn.wait_recv()

    @pl.when(jnp.logical_not(has_next))
    def _():
        dzx[0, D + T:D + T + D] = jnp.zeros((D, H), BF)

    sib_hi.start()
    columns(0, 0, D)
    columns(0, D + T, D)
    ring_start("C0")
    ring_relay("B0")
    sib_lo.wait_recv()
    sib_hi.wait_recv()
    columns(1, 0, D)
    columns(1, D + T, D)
    late = ("B1", "C1", "B2", "C2")
    for n in (0, 1, 2, 5):
        filt(n)
    ring_far("B1")
    ring_far("C1")
    ring_relay("A")
    for n in (6, 7):
        filt(n)
    ring_far("B2")
    ring_far("C2")
    ring_relay("C0")
    filt_last((0, 1, 2, 3, 4, 5, 10, 11, 12, 13, 14, 15))
    ring_far("F0")
    ring_far("F1")

    def du(lo, hi):
        @pl.loop(lo, hi)
        def _(n):
            cols = pl.ds(pl.multiple_of(256 * n, 256), 256)
            acc = jnp.zeros((T, 256), F32)
            for k in range(3):
                rows = pl.ds(pl.multiple_of(C * k + 256 * n, 256), 256)
                acc += dot_nt(dzx[0, D * (2 - k):D * (2 - k) + T], fw[rows])
            v = up32(xv[:, cols])
            ig[:, cols] = (up32(cot[0:T, cols]) + acc * slope(v, tanh_of(v))).astype(BF)

    def second(axis, q, rq, sem):
        return [remote(q.at[(pos[axis] + d) % 4], rq.at[d - 1], (sem + d - 1, sem + d - 1), at(axis, d, c))
                for d in (1, 3, 2)]

    sec_a = second("x", qa, rqa, S_P2)
    sec_f = second("x", qf, rqf, S_P2 + 3)
    sec_b = second("z", qb, rqb, S_P2 + 6)
    sec_c = second("y", qc, rqc, S_P2 + 9)

    def third(axis, t, rt, sem):
        i = pos[axis]
        out = []
        for d in (1, 3, 2):
            for cc in (0, 1):
                out.append(remote(t.at[(i + d) % 4, cc], rt.at[c, d],
                                  (sem + 4 * cc + d, sem + 4 * c + d), at(axis, d, cc)))
        out.append(remote(t.at[i, o], rt.at[c, 0], (sem + 4 * o, sem + 4 * c), sibling))
        wait = []
        for s in (0, 1):
            for d in (1, 2, 3):
                wait.append(remote(t.at[0, 0], rt.at[s, d], (sem + 4 * s + d, sem + 4 * s + d), sibling))
        wait.append(remote(t.at[0, 0], rt.at[o, 0], (sem + 4 * o, sem + 4 * o), sibling))
        return out, wait

    thr_a = third("z", ta, rta, S_P3)
    s_f = S_P3 + 8
    half = z // 2
    to_f = [[remote(tf.at[(z + d) % 4, cc], rtf.at[c, d], (s_f + 4 * cc + d, s_f + 4 * c + d), at("z", d, cc))
             for cc in (0, 1)] for d in (1, 2, 3)]
    to_sib = remote(tf.at[z, o], rtf.at[c, 0], (s_f + 4 * o, s_f + 4 * c), sibling)
    from_f = [remote(tf.at[0, 0], rtf.at[half, d], (s_f + 4 * half + d, s_f + 4 * half + d), sibling)
              for d in (1, 2, 3)]
    from_sib = remote(tf.at[0, 0], rtf.at[o, 0], (s_f + 4 * o, s_f + 4 * o), sibling)

    def each_to_f(do):
        for d in (1, 2, 3):
            @pl.when(((z + d) % 4) // 2 == c)
            def _():
                for cp in to_f[d - 1]:
                    do(cp)

    thr_b = third("y", tb, rtb, S_P3 + 16)
    thr_c = third("x", tc, rtc, S_P3 + 24)

    def begin(copies):
        for cp in copies:
            cp.start()

    def pairs(q, s):
        for p in range(3):
            for xx in range(4):
                lo = 320 * p + 40 * xx
                q[xx, 80 * p:80 * (p + 1)] = jnp.concatenate(
                    [s[lo:lo + 40], s[lo + 160:lo + 200]], axis=0).astype(BF)

    def gather(sec, q, rq, mine, s2, rows):
        for cp in sec:
            cp.wait_recv()
        r = pl.ds(0, rows)
        s2[r] = up32(q[mine, r]) + up32(rq[0, r]) + up32(rq[1, r]) + up32(rq[2, r])

    def rows36(s2, t, owners=(0, 1, 2, 3)):
        for n, owner in enumerate(owners):
            for cc in range(2):
                lo = 72 * n + 36 * cc
                t[owner, cc] = s2[lo:lo + 48].astype(BF)

    def fives(s2, t):
        for p in range(3):
            for n in range(4):
                for cc in range(2):
                    lo = 80 * p + 10 * n + 5 * cc
                    t[n, cc, 16 * p:16 * (p + 1)] = jnp.concatenate(
                        [s2[lo:lo + 8], s2[lo + 40:lo + 48]], axis=0).astype(BF)

    du(0, 1)
    for part in late:
        ring_near(part)
    ring_near("F0")
    ring_near("F1")
    du(1, 3)
    for part in late:
        ring_relay(part)
    ring_relay("F0")
    ring_relay("F1")


    s2a[240:248] = jnp.zeros((8, 128), F32)
    s2f[144:160] = jnp.zeros((16, 128), F32)
    s2b[288:304] = jnp.zeros((16, 128), F32)
    s2c[288:304] = jnp.zeros((16, 128), F32)
    def sum_pieces(p, i, rf, to, pieces):
        for first, off, rows in pieces:
            for h in range(2):
                r, f = pl.ds(first + rows * h, rows), pl.ds(off, rows)
                to[r] = up32(p[i, r]) + up32(rf[0, 1 - h, f]) + up32(rf[1, h, f])

    ring_end("A")
    sum_pieces(pa, y, rfa, sa, ((0, 0, 480),))
    pairs(qa, sa)
    begin(sec_a)

    ring_end("B0")
    ring_end("B1")
    ring_end("B2")
    sum_pieces(pb, x, rfb, sb, PIECES)
    for h in range(2):
        for zz in range(4):
            lo = 576 * h + 72 * zz
            qb[zz, 144 * h:144 * (h + 1)] = jnp.concatenate(
                [sb[lo:lo + 72], sb[lo + 288:lo + 360]], axis=0).astype(BF)
    begin(sec_b)

    ring_end("C0")
    ring_end("C1")
    ring_end("C2")
    sum_pieces(pc, z, rfc, sc, PIECES)
    for yy in range(4):
        for xp in range(2):
            lo = row_c(yy, xp)
            qc[yy, 144 * xp:144 * (xp + 1)] = sc[lo:lo + 144].astype(BF)
    begin(sec_c)

    ring_end("F0")
    ring_end("F1")
    sum_pieces(pf, y, rff, sf, PIECES_F)
    for xx in range(4):
        qf[xx] = sf[144 * xx:144 * (xx + 1)].astype(BF)
    begin(sec_f)
    du(3, 6)
    store_ig = local(ig, ig_hbm.at[0], 6)
    store_ig.start()
    gather(sec_a, qa, rqa, x, s2a, 240)
    fives(s2a, ta)
    begin(thr_a[0])
    rta[c, 0] = ta[z, c]

    mid = jnp.where(x < 2, 1, 0)
    for sec, thr, q, rq, mine, s2, t, rt, i, owners in (
            (sec_b, thr_b, qb, rqb, z, s2b, tb, rtb, y, (1 + mid, 0, 2 - mid, 3)),
            (sec_c, thr_c, qc, rqc, y, s2c, tc, rtc, x, (0, 1, 2, 3))):
        gather(sec, q, rq, mine, s2, 288)
        rows36(s2, t, owners)
        begin(thr[0])
        rt[c, 0] = t[i, c]

    gather(sec_f, qf, rqf, x, s2f, 144)
    for n in range(2):
        for cc in range(2):
            lo = 72 * n + 36 * cc
            tf[2 * c + n, cc] = s2f[lo:lo + 48].astype(BF)
    each_to_f(lambda cp: cp.start())

    @pl.when(half == c)
    def _():
        to_sib.start()
        rtf[c, 0] = tf[z, c]

    scale = 1.0 / (4 * 8192) ** 0.5

    def total(thr, rt):
        for cp in thr[1]:
            cp.wait_recv()
        return [(up32(rt[s, 0]) + up32(rt[s, 1]) + up32(rt[s, 2]) + up32(rt[s, 3])) * scale for s in range(2)]

    for s, v in enumerate(total(thr_a, rta)):
        for b in range(6):
            po_ref[:, 768 * s + 128 * b:768 * s + 128 * (b + 1)] = v[8 * b:8 * b + 5]
    for s, v in enumerate(total(thr_b, rtb)):
        fo_ref[:, 256 * s:256 * s + 128] = v[0:36]
    for s, v in enumerate(total(thr_c, rtc)):
        fo_ref[:, 256 * s + 128:256 * s + 256] = v[0:36]
    for cp in from_f:
        cp.wait_recv()

    @pl.when(half != c)
    def _():
        from_sib.wait_recv()

    last = up32(rtf[half, 0]) + up32(rtf[half, 1]) + up32(rtf[half, 2]) + up32(rtf[half, 3])
    fo_ref[:, 512:640] = (last * scale)[0:36]

    @pl.when(has_next)
    def _():
        halo_up.wait_send()
        dz_up.wait_send()

    @pl.when(has_prev)
    def _():
        halo_dn.wait_send()
        dz_dn.wait_send()

    for cp in (sib_c, sib_u, sib_g, sib_d, sib_lo, sib_hi):
        cp.wait_send()
    def ring_left(part):
        for k in (0, 1):
            for w in range(3):
                steps[part][k][w].wait_send()

    ring_left("A")
    for part in ("B0", "C0", "F0", "F1") + late:
        ring_left(part)

    each_to_f(lambda cp: cp.wait_send())

    @pl.when(half == c)
    def _():
        to_sib.wait_send()

    for cp in sec_a + sec_f + sec_b + sec_c + thr_a[0] + thr_b[0] + thr_c[0]:
        cp.wait_send()
    store_ig.wait()


def finish(*refs):
    ins, outs, held, sem = refs[:3], refs[3:6], refs[6:9], refs[9]
    come = [pltpu.make_async_copy(a, v, sem.at[i]) for i, (a, v) in enumerate(zip(ins, held))]
    go = [pltpu.make_async_copy(v, b, sem.at[3 + i]) for i, (v, b) in enumerate(zip(held, outs))]
    for cp in come:
        cp.start()
    for cp, then in zip(come, go):
        cp.wait()
        then.start()
    for cp in go:
        cp.wait()


def shards(inputs, cotangent, filter_weight, projection_weight):
    v = pltpu.VMEM
    anywhere = pl.BlockSpec(memory_space=pl.ANY)
    whole = pl.BlockSpec(memory_space=pltpu.VMEM)
    scratch = [
        v((T, C), BF), v((T, C), BF), v((2, C, T), BF), v((2 * T, C), BF), v((3 * C, H), BF), v((H, C), BF),
        v((2, D, H), BF), v((2, D, H), BF), v((T, H), F32), v((T, H), F32), v((T, H), BF),
        v((2, H, T), BF), v((2, T + 2 * D, H), BF), v((2, T + 2 * D, 384), BF),
        v((4, 960, 128), BF), v((4, 576, 128), BF), v((4, 1152, 128), BF), v((4, 1152, 128), BF),
        v((2, 480, 128), BF), v((2, 288, 128), BF), v((2, 576, 128), BF), v((2, 576, 128), BF),
        v((2, 2, 480, 128), BF), v((2, 2, 288, 128), BF), v((2, 2, 576, 128), BF), v((2, 2, 576, 128), BF),
        v((960, 128), F32), v((576, 128), F32), v((1152, 128), F32), v((1152, 128), F32),
        v((4, 240, 128), BF), v((4, 144, 128), BF), v((4, 288, 128), BF), v((4, 288, 128), BF),
        v((3, 240, 128), BF), v((3, 144, 128), BF), v((3, 288, 128), BF), v((3, 288, 128), BF),
        v((248, 128), F32), v((160, 128), F32), v((304, 128), F32), v((304, 128), F32),
        v((4, 2, 48, 128), BF), v((4, 2, 48, 128), BF), v((4, 2, 48, 128), BF), v((4, 2, 48, 128), BF),
        v((2, 4, 48, 128), BF), v((2, 4, 48, 128), BF), v((2, 4, 48, 128), BF), v((2, 4, 48, 128), BF),
        v((T, C), BF),
        pltpu.SemaphoreType.DMA((8,)), pltpu.SemaphoreType.DMA((N_SEM,)), pltpu.SemaphoreType.DMA((N_SEM,)),
    ]
    shapes = (
        jax.ShapeDtypeStruct((1, T, C), BF),
        jax.ShapeDtypeStruct((36, H), F32),
        jax.ShapeDtypeStruct((5, C), F32),
    )
    results = pl.pallas_call(
        kernel,
        name="block_backward",
        out_shape=shapes,
        in_specs=[anywhere] * 4,
        out_specs=(anywhere, whole, whole),
        scratch_shapes=scratch,
        compiler_params=pltpu.CompilerParams(
            collective_id=0, has_side_effects=True, vmem_limit_bytes=56 * 2**20),
        cost_estimate=pl.CostEstimate(flops=5_600_000_000, bytes_accessed=12_000_000, transcendentals=1_000_000),
    )(inputs, cotangent, filter_weight, projection_weight)
    return pl.pallas_call(
        finish,
        name="hand_out",
        out_shape=shapes,
        in_specs=[anywhere] * 3,
        out_specs=[anywhere] * 3,
        scratch_shapes=[v(s.shape, s.dtype) for s in shapes] + [pltpu.SemaphoreType.DMA((6,))],
    )(*results)


def solution(mesh):
    in_specs = (P("grp", "seq", None), P("grp", "seq", None), P(), P())
    out_specs = (P("grp", "seq", None), P(("seq", "grp"), None), P(("seq", "grp"), None))
    return jax.shard_map(shards, mesh=mesh, in_specs=in_specs, out_specs=out_specs, check_vma=False)
```

```python
import jax
import jax.numpy as jnp
from jax import lax
from jax.experimental import pallas as pl
from jax.experimental.pallas import tpu as pltpu
from jax.sharding import PartitionSpec as P

MESH = pl.DeviceIdType.MESH
BF, F32 = jnp.bfloat16, jnp.float32
D = 64
T = 256
C = 1536
H = 640
COEFF = 0.7978845608028654
NT = (((1,), (1,)), ((), ()))

S_HALO = 0
S_DZ = 2
S_SIB = 4
S_P1 = 10
S_P2 = 64
S_P3 = 76
N_SEM = 108


PIECES = ((0, 0, 144), (288, 144, 224), (736, 368, 208))
PIECES_F = ((0, 0, 144), (288, 144, 144))


def slot_b(xx, yy):
    if yy == (2 if xx < 2 else 1):
        return 0
    return {0: 1, 1: 2, 2: 2, 3: 3}[yy]


def row_c(yy, xp):
    return 144 * ((1, 1), (2, 0), (0, 0), (0, 1), (1, 0), (2, 1), (3, 0), (3, 1)).index((yy, xp))


def tanh_of(v):
    return jnp.tanh(COEFF * (v + 0.044715 * (v * v * v)))


def slope(v, t):
    return 0.5 * (1.0 + t) + 0.5 * v * (1.0 - t * t) * COEFF * (1.0 + 3.0 * 0.044715 * v * v)


def dot(a, b):
    return jnp.dot(a, b, preferred_element_type=F32)


def dot_nt(a, b):
    return lax.dot_general(a, b, NT, preferred_element_type=F32)


def up32(v):
    return v.astype(F32)


def kernel(x_hbm, cot_hbm, fw_hbm, pw_hbm, ig_hbm, fo_ref, po_ref,
           xv, ue, ut, cot, fw, pw, eo, ei, z_ref, dg_ref, g_ref, gt, dzx, dzc,
           pa, pf, pb, pc, rla, rlf, rlb, rlc, rfa, rff, rfb, rfc,
           sa, sf, sb, sc, qa, qf, qb, qc, rqa, rqf, rqb, rqc, s2a, s2f, s2b, s2c,
           ta, tf, tb, tc, rta, rtf, rtb, rtc, ig, lsem, ssem, rsem):
    seq, grp = lax.axis_index("seq"), lax.axis_index("grp")
    y, x, z, c = seq // 8, (seq // 2) % 4, (seq % 2) * 2 + grp // 2, grp % 2
    o = 1 - c

    def dev(xx, yy, zz, cc):
        return (yy * 8 + xx * 2 + zz // 2, (zz % 2) * 2 + cc)

    def at(axis, d, cc):
        xx = (x + d) % 4 if axis == "x" else x
        yy = (y + d) % 4 if axis == "y" else y
        zz = (z + d) % 4 if axis == "z" else z
        return dev(xx, yy, zz, cc)

    sibling = (seq, grp + 1 - 2 * c)
    pos = {"x": x, "y": y, "z": z}
    has_prev, has_next = seq > 0, seq < 31
    nxt, prv = (seq + 1, grp), (seq - 1, grp)

    def remote(src, dst, sem, device):
        return pltpu.make_async_remote_copy(
            src_ref=src, dst_ref=dst, send_sem=ssem.at[sem[0]], recv_sem=rsem.at[sem[1]],
            device_id=device, device_id_type=MESH)

    def local(src, dst, i):
        return pltpu.make_async_copy(src, dst, lsem.at[i])

    load_x = local(x_hbm.at[0], xv, 0)
    load_f = [local(fw_hbm.at[pl.ds(C * k, C)], fw.at[pl.ds(C * k, C)], 1 + k) for k in range(3)]
    load_c = local(cot_hbm.at[0], cot.at[pl.ds(0, T)], 4)
    load_p = local(pw_hbm, pw, 5)
    load_x.start()
    load_f[0].start()
    load_f[2].start()

    barrier = pltpu.get_barrier_semaphore()

    def greet(device):
        pl.semaphore_signal(barrier, inc=1, device_id=device, device_id_type=MESH)

    @pl.when(has_next)
    def _():
        greet(nxt)

    @pl.when(has_prev)
    def _():
        greet(prv)

    greet(sibling)
    for axis in ("x", "y", "z"):
        for d in (1, 2, 3):
            for cc in (0, 1):
                greet(at(axis, d, cc))

    def act(first, rows):
        v = up32(xv[pl.ds(first, rows)])
        ue[pl.ds(first, rows)] = (0.5 * v * (1.0 + tanh_of(v))).astype(BF)

    load_x.wait()
    for first in (192, 224, 0, 32):
        act(first, 32)
    pl.semaphore_wait(barrier, 19 + has_prev.astype(jnp.int32) + has_next.astype(jnp.int32))
    halo_up = remote(eo.at[0], ei.at[0], (S_HALO, S_HALO), nxt)
    halo_dn = remote(eo.at[1], ei.at[1], (S_HALO + 1, S_HALO + 1), prv)
    dz_up = remote(dzx.at[0, pl.ds(T, D)], dzx.at[0, pl.ds(0, D)], (S_DZ, S_DZ), nxt)
    dz_dn = remote(dzx.at[0, pl.ds(D, D)], dzx.at[0, pl.ds(D + T, D)], (S_DZ + 1, S_DZ + 1), prv)

    load_f[0].wait()
    eo[0] = dot(ue[T - D:T], fw[0:C]).astype(BF)

    @pl.when(has_next)
    def _():
        halo_up.start()

    load_f[2].wait()
    load_f[1].start()
    load_c.start()
    load_p.start()
    eo[1] = dot(ue[0:D], fw[2 * C:3 * C]).astype(BF)

    @pl.when(has_prev)
    def _():
        halo_dn.start()

    sib_c = remote(cot_hbm.at[0], cot.at[pl.ds(T, T)], (S_SIB, S_SIB), sibling)
    sib_u = remote(ut.at[0], ut.at[1], (S_SIB + 1, S_SIB + 1), sibling)
    sib_g = remote(gt.at[0], gt.at[1], (S_SIB + 2, S_SIB + 2), sibling)

    def sib_dz(first, rows, sem):
        return remote(dzx.at[0, pl.ds(first, rows)], dzx.at[1, pl.ds(first, rows)], (sem, sem), sibling)

    sib_d = sib_dz(D, T, S_SIB + 3)
    sib_lo = sib_dz(0, D, S_SIB + 4)
    sib_hi = sib_dz(D + T, D, S_SIB + 5)
    sib_c.start()

    @pl.loop(0, 4)
    def _(i):
        act(pl.multiple_of(D + i * 32, 32), 32)

    ut[0, :, 0:128] = ue[0:128].T
    ut[0, :, 128:256] = ue[128:256].T
    sib_u.start()

    load_f[1].wait()
    z_ref[...] = dot(ue[...], fw[C:2 * C])
    z_ref[64:256] += dot(ue[0:192], fw[0:C])
    z_ref[0:192] += dot(ue[64:256], fw[2 * C:3 * C])
    load_c.wait()
    load_p.wait()
    dg_ref[...] = dot_nt(cot[0:T], pw[...])

    def inner(first):
        rows = pl.ds(first, 32)
        v = z_ref[rows]
        t = tanh_of(v)
        g_ref[rows] = (0.5 * v * (1.0 + t)).astype(BF)
        dzx[0, pl.ds(D + first, 32)] = (dg_ref[rows] * slope(v, t)).astype(BF)

    for first in (64, 96, 128, 160):
        inner(first)

    @pl.when(has_prev)
    def _():
        halo_up.wait_recv()
        z_ref[0:64] += up32(ei[0])

    inner(0)
    inner(32)

    @pl.when(has_prev)
    def _():
        dz_dn.start()

    @pl.when(has_next)
    def _():
        halo_dn.wait_recv()
        z_ref[192:256] += up32(ei[1])

    inner(192)
    inner(224)

    @pl.when(has_next)
    def _():
        dz_up.start()

    gt[0] = g_ref[...].T
    sib_g.start()
    sib_d.start()

    def flat(p, first, rows):
        return lambda j, h: p.at[j, pl.ds(first + rows * h, rows)]

    def cut(r, first, rows):
        return r.at[..., pl.ds(first, rows), :]

    rings = {
        "A": ("y", flat(pa, 0, 480), rla, rfa, S_P1),
    }
    for n, (first, off, rows) in enumerate(PIECES_F):
        rings[f"F{n}"] = ("y", flat(pf, first, rows), cut(rlf, off, rows), cut(rff, off, rows), S_P1 + 6 + 6 * n)
    for n, (first, off, rows) in enumerate(PIECES):
        rings[f"B{n}"] = ("x", flat(pb, first, rows), cut(rlb, off, rows), cut(rfb, off, rows), S_P1 + 18 + 6 * n)
        rings[f"C{n}"] = ("z", flat(pc, first, rows), cut(rlc, off, rows), cut(rfc, off, rows), S_P1 + 36 + 6 * n)

    def ring(part):
        axis, chunk, rl, rf, sem = rings[part]
        i = pos[axis]
        up, far, dn = (i + 1) % 4, (i + 2) % 4, (i + 3) % 4
        out = []
        for k, (near, h, to) in enumerate(((up, 0, 1), (dn, 1, 3))):
            who = at(axis, to, c)
            s = sem + 3 * k
            out.append((
                remote(chunk(far, h), rl.at[k], (s, s), who),
                remote(chunk(near, 1 - h), rf.at[k, 0], (s + 1, s + 1), who),
                remote(chunk(near, h), rf.at[k, 1], (s + 2, s + 2), who),
                chunk(near, h), rl.at[k]))
        return out

    steps = {part: ring(part) for part in rings}

    def ring_far(part):
        for k in (0, 1):
            steps[part][k][0].start()

    def ring_near(part):
        for k in (0, 1):
            steps[part][k][1].start()

    def ring_start(part):
        ring_far(part)
        ring_near(part)

    def ring_relay(part):
        for k in (0, 1):
            first, _, second, mine, came = steps[part][k]
            first.wait_recv()
            mine[...] = (up32(mine[...]) + up32(came[...])).astype(BF)
            second.start()

    def ring_end(part):
        for k in (0, 1):
            steps[part][k][1].wait_recv()
            steps[part][k][2].wait_recv()

    def proj(to, first, n):
        cols = pl.ds(pl.multiple_of(first, 256), 256)
        acc = dot(gt[0], cot[0:T, cols]) + dot(gt[1], cot[T:2 * T, cols])
        for j in range(4):
            for b in range(2):
                to[j, 320 * n + 160 * b:320 * n + 160 * (b + 1)] = (
                    acc[160 * j:160 * (j + 1), 128 * b:128 * (b + 1)].astype(BF))

    sib_c.wait_recv()
    sib_g.wait_recv()
    for n in range(3):
        proj(pa, 768 * c + 256 * n, n)
    ring_far("A")

    def columns(s, first, rows):
        r = pl.ds(first, rows)
        dzc[s, r, 0:256] = dzx[s, r, pl.ds(pl.multiple_of(256 * c, 256), 256)]
        dzc[s, r, 256:384] = dzx[s, r, 512:640]

    def rhs(tap, lo, hi):
        r = pl.ds(D * (2 - tap), T)
        return jnp.concatenate([dzc[0, r, lo:hi], dzc[1, r, lo:hi]], axis=0)

    def rows_of(first, rows, lo, hi):
        out = []
        last = first + rows
        while first < last:
            tap = first // C
            stop = min(last, C * (tap + 1))
            r = slice(first - C * tap, stop - C * tap)
            left = jnp.concatenate([ut[0, r], ut[1, r]], axis=1)
            out.append(dot(left, rhs(tap, lo, hi)))
            first = stop
        return out[0] if len(out) == 1 else jnp.concatenate(out, axis=0)

    def filt(n):
        yy, xp = n // 2, n % 2
        acc = rows_of(576 * n, 576, 0, 256)
        for b in range(2):
            first = 288 * slot_b(2 * xp + b, yy)
            pb[2 * xp + b, first:first + 288] = acc[288 * b:288 * (b + 1), 0:128].astype(BF)
        first = row_c(yy, xp)
        for zz in range(4):
            pc[zz, first:first + 144] = jnp.concatenate(
                [acc[72 * zz:72 * zz + 72, 128:256], acc[288 + 72 * zz:360 + 72 * zz, 128:256]],
                axis=0).astype(BF)

    def filt_last(groups):
        for core in range(2):
            @pl.when(c == core)
            def _():
                for n in groups:
                    pf[n // 4, 144 * (n % 4):144 * (n % 4 + 1)] = (
                        rows_of(288 * n + 144 * core, 144, 256, 384).astype(BF))

    columns(0, D, T)
    sib_u.wait_recv()
    sib_d.wait_recv()
    columns(1, D, T)
    filt(3)
    filt(4)
    ring_start("B0")
    ring_near("A")
    filt_last((6, 7, 8, 9))
    @pl.when(has_prev)
    def _():
        dz_up.wait_recv()

    @pl.when(jnp.logical_not(has_prev))
    def _():
        dzx[0, 0:D] = jnp.zeros((D, H), BF)

    sib_lo.start()

    @pl.when(has_next)
    def _():
        dz_dn.wait_recv()

    @pl.when(jnp.logical_not(has_next))
    def _():
        dzx[0, D + T:D + T + D] = jnp.zeros((D, H), BF)

    sib_hi.start()
    columns(0, 0, D)
    columns(0, D + T, D)
    ring_start("C0")
    ring_relay("B0")
    sib_lo.wait_recv()
    sib_hi.wait_recv()
    columns(1, 0, D)
    columns(1, D + T, D)
    late = ("B1", "C1", "B2", "C2")
    for n in (0, 1, 2, 5):
        filt(n)
    ring_far("B1")
    ring_far("C1")
    ring_relay("A")
    for n in (6, 7):
        filt(n)
    ring_far("B2")
    ring_far("C2")
    ring_relay("C0")
    filt_last((0, 1, 2, 3, 4, 5, 10, 11, 12, 13, 14, 15))
    ring_far("F0")
    ring_far("F1")

    def du(lo, hi):
        @pl.loop(lo, hi)
        def _(n):
            cols = pl.ds(pl.multiple_of(256 * n, 256), 256)
            acc = jnp.zeros((T, 256), F32)
            for k in range(3):
                rows = pl.ds(pl.multiple_of(C * k + 256 * n, 256), 256)
                acc += dot_nt(dzx[0, D * (2 - k):D * (2 - k) + T], fw[rows])
            v = up32(xv[:, cols])
            ig[:, cols] = (up32(cot[0:T, cols]) + acc * slope(v, tanh_of(v))).astype(BF)

    def second(axis, q, rq, sem):
        return [remote(q.at[(pos[axis] + d) % 4], rq.at[d - 1], (sem + d - 1, sem + d - 1), at(axis, d, c))
                for d in (1, 2, 3)]

    sec_a = second("x", qa, rqa, S_P2)
    sec_f = second("x", qf, rqf, S_P2 + 3)
    sec_b = second("z", qb, rqb, S_P2 + 6)
    sec_c = second("y", qc, rqc, S_P2 + 9)

    def third(axis, t, rt, sem):
        i = pos[axis]
        out = []
        for d in (2, 1, 3):
            for cc in (0, 1):
                out.append(remote(t.at[(i + d) % 4, cc], rt.at[c, d],
                                  (sem + 4 * cc + d, sem + 4 * c + d), at(axis, d, cc)))
        out.append(remote(t.at[i, o], rt.at[c, 0], (sem + 4 * o, sem + 4 * c), sibling))
        wait = []
        for s in (0, 1):
            for d in (1, 2, 3):
                wait.append(remote(t.at[0, 0], rt.at[s, d], (sem + 4 * s + d, sem + 4 * s + d), sibling))
        wait.append(remote(t.at[0, 0], rt.at[o, 0], (sem + 4 * o, sem + 4 * o), sibling))
        return out, wait

    thr_a = third("z", ta, rta, S_P3)
    s_f = S_P3 + 8
    half = z // 2
    to_f = [[remote(tf.at[(z + d) % 4, cc], rtf.at[c, d], (s_f + 4 * cc + d, s_f + 4 * c + d), at("z", d, cc))
             for cc in (0, 1)] for d in (1, 2, 3)]
    to_sib = remote(tf.at[z, o], rtf.at[c, 0], (s_f + 4 * o, s_f + 4 * c), sibling)
    from_f = [remote(tf.at[0, 0], rtf.at[half, d], (s_f + 4 * half + d, s_f + 4 * half + d), sibling)
              for d in (1, 2, 3)]
    from_sib = remote(tf.at[0, 0], rtf.at[o, 0], (s_f + 4 * o, s_f + 4 * o), sibling)

    def each_to_f(do):
        for d in (1, 2, 3):
            @pl.when(((z + d) % 4) // 2 == c)
            def _():
                for cp in to_f[d - 1]:
                    do(cp)

    thr_b = third("y", tb, rtb, S_P3 + 16)
    thr_c = third("x", tc, rtc, S_P3 + 24)

    def begin(copies):
        for cp in copies:
            cp.start()

    def pairs(q, s):
        for p in range(3):
            for xx in range(4):
                lo = 320 * p + 40 * xx
                q[xx, 80 * p:80 * (p + 1)] = jnp.concatenate(
                    [s[lo:lo + 40], s[lo + 160:lo + 200]], axis=0).astype(BF)

    def gather(sec, q, rq, mine, s2, rows):
        for cp in sec:
            cp.wait_recv()
        r = pl.ds(0, rows)
        s2[r] = up32(q[mine, r]) + up32(rq[0, r]) + up32(rq[1, r]) + up32(rq[2, r])

    def rows36(s2, t, owners=(0, 1, 2, 3)):
        for n, owner in enumerate(owners):
            for cc in range(2):
                lo = 72 * n + 36 * cc
                t[owner, cc] = s2[lo:lo + 48].astype(BF)

    def fives(s2, t):
        for p in range(3):
            for n in range(4):
                for cc in range(2):
                    lo = 80 * p + 10 * n + 5 * cc
                    t[n, cc, 16 * p:16 * (p + 1)] = jnp.concatenate(
                        [s2[lo:lo + 8], s2[lo + 40:lo + 48]], axis=0).astype(BF)

    du(0, 2)
    for part in late:
        ring_near(part)
    ring_near("F0")
    ring_near("F1")
    du(2, 3)
    for part in late:
        ring_relay(part)
    ring_relay("F0")
    ring_relay("F1")


    s2a[240:248] = jnp.zeros((8, 128), F32)
    s2f[144:160] = jnp.zeros((16, 128), F32)
    s2b[288:304] = jnp.zeros((16, 128), F32)
    s2c[288:304] = jnp.zeros((16, 128), F32)
    def sum_pieces(p, i, rf, to, pieces):
        for first, off, rows in pieces:
            for h in range(2):
                r, f = pl.ds(first + rows * h, rows), pl.ds(off, rows)
                to[r] = up32(p[i, r]) + up32(rf[0, 1 - h, f]) + up32(rf[1, h, f])

    ring_end("A")
    sum_pieces(pa, y, rfa, sa, ((0, 0, 480),))
    pairs(qa, sa)
    begin(sec_a)

    ring_end("B0")
    ring_end("B1")
    ring_end("B2")
    sum_pieces(pb, x, rfb, sb, PIECES)
    for h in range(2):
        for zz in range(4):
            lo = 576 * h + 72 * zz
            qb[zz, 144 * h:144 * (h + 1)] = jnp.concatenate(
                [sb[lo:lo + 72], sb[lo + 288:lo + 360]], axis=0).astype(BF)
    begin(sec_b)

    ring_end("C0")
    ring_end("C1")
    ring_end("C2")
    sum_pieces(pc, z, rfc, sc, PIECES)
    for yy in range(4):
        for xp in range(2):
            lo = row_c(yy, xp)
            qc[yy, 144 * xp:144 * (xp + 1)] = sc[lo:lo + 144].astype(BF)
    begin(sec_c)

    ring_end("F0")
    ring_end("F1")
    sum_pieces(pf, y, rff, sf, PIECES_F)
    for xx in range(4):
        qf[xx] = sf[144 * xx:144 * (xx + 1)].astype(BF)
    begin(sec_f)
    du(3, 6)
    store_ig = local(ig, ig_hbm.at[0], 6)
    store_ig.start()
    gather(sec_a, qa, rqa, x, s2a, 240)
    fives(s2a, ta)
    begin(thr_a[0])
    rta[c, 0] = ta[z, c]

    mid = jnp.where(x < 2, 1, 0)
    for sec, thr, q, rq, mine, s2, t, rt, i, owners in (
            (sec_b, thr_b, qb, rqb, z, s2b, tb, rtb, y, (1 + mid, 0, 2 - mid, 3)),
            (sec_c, thr_c, qc, rqc, y, s2c, tc, rtc, x, (0, 1, 2, 3))):
        gather(sec, q, rq, mine, s2, 288)
        rows36(s2, t, owners)
        begin(thr[0])
        rt[c, 0] = t[i, c]

    gather(sec_f, qf, rqf, x, s2f, 144)
    for n in range(2):
        for cc in range(2):
            lo = 72 * n + 36 * cc
            tf[2 * c + n, cc] = s2f[lo:lo + 48].astype(BF)
    each_to_f(lambda cp: cp.start())

    @pl.when(half == c)
    def _():
        to_sib.start()
        rtf[c, 0] = tf[z, c]

    scale = 1.0 / (4 * 8192) ** 0.5

    def total(thr, rt):
        for cp in thr[1]:
            cp.wait_recv()
        return [(up32(rt[s, 0]) + up32(rt[s, 1]) + up32(rt[s, 2]) + up32(rt[s, 3])) * scale for s in range(2)]

    for s, v in enumerate(total(thr_a, rta)):
        for b in range(6):
            po_ref[:, 768 * s + 128 * b:768 * s + 128 * (b + 1)] = v[8 * b:8 * b + 5]
    for s, v in enumerate(total(thr_b, rtb)):
        fo_ref[:, 256 * s:256 * s + 128] = v[0:36]
    for s, v in enumerate(total(thr_c, rtc)):
        fo_ref[:, 256 * s + 128:256 * s + 256] = v[0:36]
    for cp in from_f:
        cp.wait_recv()

    @pl.when(half != c)
    def _():
        from_sib.wait_recv()

    last = up32(rtf[half, 0]) + up32(rtf[half, 1]) + up32(rtf[half, 2]) + up32(rtf[half, 3])
    fo_ref[:, 512:640] = (last * scale)[0:36]

    @pl.when(has_next)
    def _():
        halo_up.wait_send()
        dz_up.wait_send()

    @pl.when(has_prev)
    def _():
        halo_dn.wait_send()
        dz_dn.wait_send()

    for cp in (sib_c, sib_u, sib_g, sib_d, sib_lo, sib_hi):
        cp.wait_send()
    def ring_left(part):
        for k in (0, 1):
            for w in range(3):
                steps[part][k][w].wait_send()

    ring_left("A")
    for part in ("B0", "C0", "F0", "F1") + late:
        ring_left(part)

    each_to_f(lambda cp: cp.wait_send())

    @pl.when(half == c)
    def _():
        to_sib.wait_send()

    for cp in sec_a + sec_f + sec_b + sec_c + thr_a[0] + thr_b[0] + thr_c[0]:
        cp.wait_send()
    store_ig.wait()


def finish(*refs):
    ins, outs, held, sem = refs[:3], refs[3:6], refs[6:9], refs[9]
    come = [pltpu.make_async_copy(a, v, sem.at[i]) for i, (a, v) in enumerate(zip(ins, held))]
    go = [pltpu.make_async_copy(v, b, sem.at[3 + i]) for i, (v, b) in enumerate(zip(held, outs))]
    for cp in come:
        cp.start()
    for cp, then in zip(come, go):
        cp.wait()
        then.start()
    for cp in go:
        cp.wait()


def shards(inputs, cotangent, filter_weight, projection_weight):
    v = pltpu.VMEM
    anywhere = pl.BlockSpec(memory_space=pl.ANY)
    whole = pl.BlockSpec(memory_space=pltpu.VMEM)
    scratch = [
        v((T, C), BF), v((T, C), BF), v((2, C, T), BF), v((2 * T, C), BF), v((3 * C, H), BF), v((H, C), BF),
        v((2, D, H), BF), v((2, D, H), BF), v((T, H), F32), v((T, H), F32), v((T, H), BF),
        v((2, H, T), BF), v((2, T + 2 * D, H), BF), v((2, T + 2 * D, 384), BF),
        v((4, 960, 128), BF), v((4, 576, 128), BF), v((4, 1152, 128), BF), v((4, 1152, 128), BF),
        v((2, 480, 128), BF), v((2, 288, 128), BF), v((2, 576, 128), BF), v((2, 576, 128), BF),
        v((2, 2, 480, 128), BF), v((2, 2, 288, 128), BF), v((2, 2, 576, 128), BF), v((2, 2, 576, 128), BF),
        v((960, 128), F32), v((576, 128), F32), v((1152, 128), F32), v((1152, 128), F32),
        v((4, 240, 128), BF), v((4, 144, 128), BF), v((4, 288, 128), BF), v((4, 288, 128), BF),
        v((3, 240, 128), BF), v((3, 144, 128), BF), v((3, 288, 128), BF), v((3, 288, 128), BF),
        v((248, 128), F32), v((160, 128), F32), v((304, 128), F32), v((304, 128), F32),
        v((4, 2, 48, 128), BF), v((4, 2, 48, 128), BF), v((4, 2, 48, 128), BF), v((4, 2, 48, 128), BF),
        v((2, 4, 48, 128), BF), v((2, 4, 48, 128), BF), v((2, 4, 48, 128), BF), v((2, 4, 48, 128), BF),
        v((T, C), BF),
        pltpu.SemaphoreType.DMA((8,)), pltpu.SemaphoreType.DMA((N_SEM,)), pltpu.SemaphoreType.DMA((N_SEM,)),
    ]
    shapes = (
        jax.ShapeDtypeStruct((1, T, C), BF),
        jax.ShapeDtypeStruct((36, H), F32),
        jax.ShapeDtypeStruct((5, C), F32),
    )
    results = pl.pallas_call(
        kernel,
        name="block_backward",
        out_shape=shapes,
        in_specs=[anywhere] * 4,
        out_specs=(anywhere, whole, whole),
        scratch_shapes=scratch,
        compiler_params=pltpu.CompilerParams(
            collective_id=0, has_side_effects=True, vmem_limit_bytes=56 * 2**20),
        cost_estimate=pl.CostEstimate(flops=5_600_000_000, bytes_accessed=12_000_000, transcendentals=1_000_000),
    )(inputs, cotangent, filter_weight, projection_weight)
    return pl.pallas_call(
        finish,
        name="hand_out",
        out_shape=shapes,
        in_specs=[anywhere] * 3,
        out_specs=[anywhere] * 3,
        scratch_shapes=[v(s.shape, s.dtype) for s in shapes] + [pltpu.SemaphoreType.DMA((6,))],
    )(*results)


def solution(mesh):
    in_specs = (P("grp", "seq", None), P("grp", "seq", None), P(), P())
    out_specs = (P("grp", "seq", None), P(("seq", "grp"), None), P(("seq", "grp"), None))
    return jax.shard_map(shards, mesh=mesh, in_specs=in_specs, out_specs=out_specs, check_vma=False)
```
